1024 devices in a mesh: lon: 32 (over z_hi, y, core), lat: 32 (over x, z_lo).
Axes of the slice: x: 4, y: 4, z: 32 (z_hi: 4, z_lo: 8; z = z_hi * 8 + z_lo), core: 2. Of those that a mesh axis runs over, the one named last changes fastest.
Arguments:
- bottom_stratum_count: int32 [256, 4096], P('lat', 'lon'), may hold values from 0 to 32, as said below
- free_elevation: float32 [256, 4096], P('lat', 'lon'), may hold values from -4 to 4
- barotropic_velocity_x: float32 [256, 4096], P('lat', 'lon'), may hold values from -4 to 4
- barotropic_velocity_y: float32 [256, 4096], P('lat', 'lon'), may hold values from -4 to 4
- velocity_along_x: float32 [32, 256, 4096], P(None, 'lat', 'lon'), may hold values from -4 to 4
- velocity_along_y: float32 [32, 256, 4096], P(None, 'lat', 'lon'), may hold values from -4 to 4
- thermal_anomaly: float32 [32, 256, 4096], P(None, 'lat', 'lon'), may hold values from -6 to 6
- haline_anomaly: float32 [32, 256, 4096], P(None, 'lat', 'lon'), may hold values from -6 to 6
Outputs:
- surface_out: float32 [256, 4096], P('lat', 'lon')
- east_out: float32 [256, 4096], P('lat', 'lon')
- north_out: float32 [256, 4096], P('lat', 'lon')
- fresh_velocity_along_x: float32 [32, 256, 4096], P(None, 'lat', 'lon')
- fresh_velocity_along_y: float32 [32, 256, 4096], P(None, 'lat', 'lon')
- fresh_thermal_anomaly: float32 [32, 256, 4096], P(None, 'lat', 'lon')
- fresh_haline_anomaly: float32 [32, 256, 4096], P(None, 'lat', 'lon')
The draws below stay inside these ranges and needn't reach their ends.
Inputs may be any that keep to these rules, and one draw needn't show every extreme that they name: `bottom_stratum_count`: about three in twenty columns are land (0); the others hold 1 to 32 wet levels, independently from column to column.
All inputs are finite; a program needn't handle non-finite values.
Results may differ from the reference program's by a relative error of at most 0.00002.
Values sent between devices are 32-bit elements; how exact they have to be, the bound alone decides.
A program may use at most 32 MiB of HBM per device.

```python
import jax
import jax.numpy as jnp

STRATA_COUNT = 32
SUBCYCLES = 8
PARALLEL_COUNT = 256
MERIDIAN_COUNT = 4096


def draw_bottom_stratum_count(key, part):
    key = jax.random.fold_in(key, 11)
    land_key, depth_key = jax.random.split(key)
    landed = jax.random.randint(land_key, (PARALLEL_COUNT, MERIDIAN_COUNT), 0, 20) < 3
    levels_wet = jax.random.randint(depth_key, (PARALLEL_COUNT, MERIDIAN_COUNT), 1, STRATA_COUNT + 1)
    column = jnp.where(landed, 0, levels_wet).astype(jnp.int32)
    return column.at[0, 0].set(0).at[1, 1].set(STRATA_COUNT)


def level_of(rng, shape, cuts, low, largest):
    def one(position, blocks):
        steps = jax.random.uniform(jax.random.fold_in(jax.random.fold_in(rng, 6), position), (blocks,), jnp.float32, low / len(cuts), largest / len(cuts))
        return jnp.repeat(jnp.exp(steps), shape[position] // blocks).reshape((-1,) + (1,) * (len(shape) - position - 1))

    gain = one(*cuts[0])
    for cut in cuts[1:]:
        gain = gain * one(*cut)
    return gain


def scatter_about(rng, shape, width, bound, cuts=(), kind=jnp.bfloat16):
    values = width * jax.random.normal(rng, shape, jnp.float32)
    if cuts:
        values = values * level_of(rng, shape, cuts, -0.22, 0.18)
    return jnp.clip(values, -bound, bound).astype(kind)


def setup_inputs(seed: int = 0) -> dict:
    arg_keys = jax.random.split(jax.random.key(seed), 9)
    bottom_stratum_count = draw_bottom_stratum_count(jax.random.fold_in(arg_keys[8], 71), 0)
    free_elevation = scatter_about(arg_keys[1], (PARALLEL_COUNT, MERIDIAN_COUNT), 0.5, 4.0, ((0, 32), (1, 32)), jnp.float32)
    barotropic_velocity_x = scatter_about(arg_keys[2], (PARALLEL_COUNT, MERIDIAN_COUNT), 0.5, 4.0, ((0, 32), (1, 32)), jnp.float32)
    barotropic_velocity_y = scatter_about(arg_keys[3], (PARALLEL_COUNT, MERIDIAN_COUNT), 0.5, 4.0, ((0, 32), (1, 32)), jnp.float32)
    velocity_along_x = scatter_about(arg_keys[4], (STRATA_COUNT, PARALLEL_COUNT, MERIDIAN_COUNT), 0.5, 4.0, ((1, 32), (2, 32)), jnp.float32)
    velocity_along_y = scatter_about(arg_keys[5], (STRATA_COUNT, PARALLEL_COUNT, MERIDIAN_COUNT), 0.5, 4.0, ((1, 32), (2, 32)), jnp.float32)
    thermal_anomaly = scatter_about(arg_keys[6], (STRATA_COUNT, PARALLEL_COUNT, MERIDIAN_COUNT), 1.0, 6.0, ((1, 32), (2, 32)), jnp.float32)
    haline_anomaly = scatter_about(arg_keys[7], (STRATA_COUNT, PARALLEL_COUNT, MERIDIAN_COUNT), 1.0, 6.0, ((1, 32), (2, 32)), jnp.float32)
    return dict(bottom_stratum_count=bottom_stratum_count, free_elevation=free_elevation, barotropic_velocity_x=barotropic_velocity_x, barotropic_velocity_y=barotropic_velocity_y, velocity_along_x=velocity_along_x, velocity_along_y=velocity_along_y, thermal_anomaly=thermal_anomaly, haline_anomaly=haline_anomaly)


wave_coef = 0.45
coriolis = 0.12
diapycnal_factor = 0.2
press_coef = 0.1


def shift_east(field):
    return jnp.roll(field, -1, axis=-1)


def shift_west(field):
    return jnp.roll(field, 1, axis=-1)


def shift_north(field):
    zeros = jnp.zeros_like(field[..., :1, :])
    return jnp.concatenate([field[..., 1:, :], zeros], axis=-2)


def shift_south(field):
    zeros = jnp.zeros_like(field[..., :1, :])
    return jnp.concatenate([zeros, field[..., :-1, :]], axis=-2)


def level_above(field):
    return jnp.concatenate([jnp.zeros_like(field[:1]), field[:-1]], axis=0)


def level_below(field):
    return jnp.concatenate([field[1:], jnp.zeros_like(field[:1])], axis=0)


def reference(bottom_stratum_count, free_elevation, barotropic_velocity_x, barotropic_velocity_y, velocity_along_x, velocity_along_y, thermal_anomaly, haline_anomaly):
    depth = bottom_stratum_count.astype(jnp.float32) / STRATA_COUNT
    wet = (bottom_stratum_count > 0).astype(jnp.float32)
    stratum_index, volume_flux_x_side, volume_flux_y_side = free_elevation, barotropic_velocity_x, barotropic_velocity_y
    for cycle in range(SUBCYCLES):
        flux_x = depth * volume_flux_x_side
        flux_y = depth * volume_flux_y_side
        stratum_index = wet * (stratum_index - wave_coef * (shift_east(flux_x) - shift_west(flux_x) + shift_north(flux_y) - shift_south(flux_y)))
        new_x = wet * (volume_flux_x_side - wave_coef * depth * (shift_east(stratum_index) - shift_west(stratum_index)) + coriolis * volume_flux_y_side)
        new_y = wet * (volume_flux_y_side - wave_coef * depth * (shift_north(stratum_index) - shift_south(stratum_index)) - coriolis * volume_flux_x_side)
        volume_flux_x_side, volume_flux_y_side = new_x, new_y
    levels = jnp.arange(STRATA_COUNT, dtype=jnp.int32)[:, None, None]
    ocean_cell_indicator = (levels < bottom_stratum_count[None]).astype(jnp.float32)
    multiplier_factor = 0.08 + 0.12 * depth

    def horizontal_diffusion(field):
        total = shift_east(ocean_cell_indicator) * (shift_east(field) - field) + shift_west(ocean_cell_indicator) * (shift_west(field) - field)
        return total + shift_north(ocean_cell_indicator) * (shift_north(field) - field) + shift_south(ocean_cell_indicator) * (shift_south(field) - field)

    def diapycnal_diffusion(field):
        return level_above(ocean_cell_indicator) * (level_above(field) - field) + level_below(ocean_cell_indicator) * (level_below(field) - field)

    fresh_thermal_anomaly = ocean_cell_indicator * (thermal_anomaly + multiplier_factor * horizontal_diffusion(thermal_anomaly) + diapycnal_factor * diapycnal_diffusion(thermal_anomaly))
    fresh_haline_anomaly = ocean_cell_indicator * (haline_anomaly + multiplier_factor * horizontal_diffusion(haline_anomaly) + diapycnal_factor * diapycnal_diffusion(haline_anomaly))
    hydrostatic_force = jnp.cumsum(ocean_cell_indicator * (-0.8 * thermal_anomaly + 0.6 * haline_anomaly), axis=0)
    count = jnp.maximum(bottom_stratum_count, 1).astype(jnp.float32)
    mean_x = jnp.sum(ocean_cell_indicator * velocity_along_x, axis=0) / count
    mean_y = jnp.sum(ocean_cell_indicator * velocity_along_y, axis=0) / count
    fresh_velocity_along_x = ocean_cell_indicator * (velocity_along_x - mean_x + volume_flux_x_side + multiplier_factor * horizontal_diffusion(velocity_along_x) - press_coef * (shift_east(hydrostatic_force) - shift_west(hydrostatic_force)) + coriolis * velocity_along_y)
    fresh_velocity_along_y = ocean_cell_indicator * (velocity_along_y - mean_y + volume_flux_y_side + multiplier_factor * horizontal_diffusion(velocity_along_y) - press_coef * (shift_north(hydrostatic_force) - shift_south(hydrostatic_force)) - coriolis * velocity_along_x)
    return (stratum_index, volume_flux_x_side, volume_flux_y_side, fresh_velocity_along_x, fresh_velocity_along_y, fresh_thermal_anomaly, fresh_haline_anomaly)
```

```python
import functools

import jax
import jax.numpy as jnp
from jax import lax
from jax.experimental import pallas as pl
from jax.experimental.pallas import tpu as pltpu
from jax.sharding import PartitionSpec as P

LEVELS = 32
SUBCYCLES = 8
ROWS = 8
COLS = 128
EDGE = 16
WAVE = 0.45
CORIOLIS = 0.12
DIAPYCNAL = 0.2
UNROLL = 4

SIDES = [(a, o) for o in (-1, 1) for a in (-2, -1, 0, 1, 2)]
STACKS = [(a, 0) for a in (-2, -1, 1, 2)]
OFFSETS = SIDES + STACKS
f32 = jnp.float32


def kernel(
    bottom_hbm, level_hbm, flow_x_hbm, flow_y_hbm, x_hbm, y_hbm, t_hbm, s_hbm,
    level_out, east_out, north_out, x_out, y_out, t_out, s_out,
    bottom, own, big, edge, side_recv, stack_recv,
    row_first, row_last, row_north, row_south,
    col_to_east, col_to_west, col_from_west, col_from_east,
    local_sem, send_sem, recv_sem,
):
    lat, lon = lax.axis_index("lat"), lax.axis_index("lon")
    lats, lons = lax.axis_size("lat"), lax.axis_size("lon")

    def place(offset):
        return {
            "lat": lax.rem(lat + offset[0] + lats, lats),
            "lon": lax.rem(lon + offset[1] + lons, lons),
        }

    barrier = pltpu.get_barrier_semaphore()
    for offset in OFFSETS:
        pl.semaphore_signal(
            barrier, inc=1, device_id=place(offset), device_id_type=pl.DeviceIdType.MESH
        )

    small = [
        pltpu.make_async_copy(bottom_hbm, bottom, local_sem.at[0]),
        pltpu.make_async_copy(level_hbm, own.at[1], local_sem.at[1]),
        pltpu.make_async_copy(flow_x_hbm, own.at[2], local_sem.at[2]),
        pltpu.make_async_copy(flow_y_hbm, own.at[3], local_sem.at[3]),
    ]
    large = [
        pltpu.make_async_copy(ref, big.at[i], local_sem.at[4 + i])
        for i, ref in enumerate((x_hbm, y_hbm, t_hbm, s_hbm))
    ]
    for copy in small + large:
        copy.start()

    lane = lax.broadcasted_iota(jnp.int32, (ROWS, COLS), 1)
    row = lax.broadcasted_iota(jnp.int32, (ROWS, COLS), 0)
    even = lane % 2 == 0

    def roll(cells, shift):
        return pltpu.roll(cells, shift % COLS, 1)

    def slide(cells, shift):
        return pltpu.roll(cells, shift % ROWS, 0)

    for copy in small:
        copy.wait()
    own[0] = bottom[...].astype(f32)
    packed = roll(own[0], EDGE)
    for i in range(1, 4):
        packed = jnp.where(lane // 32 == i, roll(own[i], EDGE + 32 * i), packed)
    edge[...] = packed

    for copy in large:
        copy.wait()
    for i in range(4):
        row_first[pl.ds(i * LEVELS, LEVELS), :] = big[i, :, 0, :]
        row_last[pl.ds(i * LEVELS, LEVELS), :] = big[i, :, ROWS - 1, :]

    def pack(k, carry):
        first, second = carry
        first = jnp.where(lane // 2 == k, pltpu.roll(big[0, k], 2 * k + 1, 1), first)
        first = jnp.where(lane // 2 == k + 32, pltpu.roll(big[1, k], 2 * k + 65, 1), first)
        second = jnp.where(lane // 2 == k, pltpu.roll(big[2, k], 2 * k + 1, 1), second)
        second = jnp.where(
            lane // 2 == k + 32, pltpu.roll(big[3, k], (2 * k + 65) % COLS, 1), second
        )
        return first, second

    zero = jnp.zeros((ROWS, COLS), f32)
    first, second = lax.fori_loop(0, LEVELS, pack, (zero, zero), unroll=LEVELS)
    col_to_east[...] = jnp.where(even, first, roll(second, 1))
    col_to_west[...] = jnp.where(even, roll(first, -1), second)

    pl.semaphore_wait(barrier, len(OFFSETS))

    copies = []

    def send(src, dst, index, offset):
        copy = pltpu.make_async_remote_copy(
            src_ref=src,
            dst_ref=dst,
            send_sem=send_sem.at[index],
            recv_sem=recv_sem.at[index],
            device_id=place(offset),
            device_id_type=pl.DeviceIdType.MESH,
        )
        copy.start()
        copies.append(copy)

    for a, o in SIDES:
        slot = SIDES.index((-a, -o))
        send(edge, side_recv.at[slot], slot, (a, o))
    for a, o in STACKS:
        slot = STACKS.index((-a, -o))
        send(own, stack_recv.at[slot], len(SIDES) + slot, (a, o))
    halo_count = len(OFFSETS)
    send(col_to_east, col_from_west, halo_count, (0, 1))
    send(col_to_west, col_from_east, halo_count + 1, (0, -1))
    send(row_last, row_south, halo_count + 2, (1, 0))
    send(row_first, row_north, halo_count + 3, (-1, 0))

    centre = own[0]
    coef = 0.08 + (0.12 / LEVELS) * centre
    bottom_e = jnp.where(lane == COLS - 1, 0.0, roll(centre, -1))
    bottom_w = jnp.where(lane == 0, 0.0, roll(centre, 1))
    bottom_n = jnp.where(row == ROWS - 1, 0.0, slide(centre, -1))
    bottom_s = jnp.where(row == 0, 0.0, slide(centre, 1))

    def inner(k, carry):
        press, sum_x, sum_y = carry
        depth = lax.convert_element_type(k, f32)
        wet = centre > depth
        wet_e, wet_w = bottom_e > depth, bottom_w > depth
        wet_n, wet_s = bottom_n > depth, bottom_s > depth

        def lateral(cells):
            return (
                jnp.where(wet_e, roll(cells, -1), cells)
                + jnp.where(wet_w, roll(cells, 1), cells)
                + jnp.where(wet_n, slide(cells, -1), cells)
                + jnp.where(wet_s, slide(cells, 1), cells)
                - 4.0 * cells
            )

        x, y, t, s = big[0, k], big[1, k], big[2, k], big[3, k]
        press = press + jnp.where(wet, 0.6 * s - 0.8 * t, 0.0)
        press_x = jnp.where(lane == COLS - 1, 0.0, roll(press, -1)) - jnp.where(
            lane == 0, 0.0, roll(press, 1)
        )
        press_y = jnp.where(row == ROWS - 1, 0.0, slide(press, -1)) - jnp.where(
            row == 0, 0.0, slide(press, 1)
        )
        x_out[k] = x + coef * lateral(x) + CORIOLIS * y - 0.1 * press_x
        y_out[k] = y + coef * lateral(y) - CORIOLIS * x - 0.1 * press_y
        below = centre > depth + 1.0
        up, down = lax.max(k - 1, 0), lax.min(k + 1, LEVELS - 1)
        for i, cells, out in ((2, t, t_out), (3, s, s_out)):
            vertical = (big[i, up] - cells) + jnp.where(below, big[i, down] - cells, 0.0)
            out[k] = cells + coef * lateral(cells) + DIAPYCNAL * vertical
        return press, sum_x + jnp.where(wet, x, 0.0), sum_y + jnp.where(wet, y, 0.0)

    _, sum_x, sum_y = lax.fori_loop(0, LEVELS, inner, (zero, zero, zero), unroll=UNROLL)
    count = jnp.maximum(centre, 1.0)
    mean_x, mean_y = sum_x / count, sum_y / count

    for copy in copies[:halo_count]:
        copy.wait_recv()

    fields = [[], [], [], []]
    for a in (-2, -1, 0, 1, 2):
        inside = (lat + a >= 0) & (lat + a < lats)
        keep = jnp.where(inside, 1.0, 0.0).astype(f32)
        merged = jnp.where(
            lane % 32 < EDGE, side_recv[SIDES.index((a, -1))], side_recv[SIDES.index((a, 1))]
        )
        for i in range(4):
            middle = own[i] if a == 0 else stack_recv[STACKS.index((a, 0)), i]
            beside = roll(merged, -(EDGE + 32 * i))
            if i == 0 and a != 0:
                middle, beside = middle * keep, beside * keep
            fields[i].append((middle, beside))
    halo_bottom = fields[0]

    def whole(tiles):
        return jnp.concatenate(
            [jnp.concatenate([m for m, _ in tiles], 0), jnp.concatenate([b for _, b in tiles], 0)], 1
        )

    def ew(cells):
        return pltpu.roll(cells, 2 * COLS - 1, 1) - pltpu.roll(cells, 1, 1)

    def ns(cells):
        return pltpu.roll(cells, cells.shape[0] - 1, 0) - pltpu.roll(cells, 1, 0)

    column, level, flow_x, flow_y = (whole(tiles) for tiles in fields)
    wet = jnp.where(column > 0.0, 1.0, 0.0)
    gain = (WAVE / LEVELS) * column
    level, flow_x, flow_y = wet * level, wet * flow_x, wet * flow_y
    for cycle in range(SUBCYCLES):
        level = level - wet * (ew(gain * flow_x) + ns(gain * flow_y))
        flow_x, flow_y = (
            flow_x - gain * ew(level) + CORIOLIS * flow_y,
            flow_y - gain * ns(level) - CORIOLIS * flow_x,
        )
        if cycle == 3:
            wet, gain, level, flow_x, flow_y = (
                cells[ROWS : 4 * ROWS] for cells in (wet, gain, level, flow_x, flow_y)
            )
    level, flow_x, flow_y = (cells[ROWS : 2 * ROWS, :COLS] for cells in (level, flow_x, flow_y))
    level_out[...] = level
    east_out[...] = flow_x
    north_out[...] = flow_y

    for copy in copies[halo_count:]:
        copy.wait_recv()

    beside = halo_bottom[2][1]
    bottom_ew = jnp.where(
        lane == COLS - 1, roll(beside, -1), jnp.where(lane == 0, roll(beside, 1), 0.0)
    )
    bottom_ns = jnp.where(
        row == ROWS - 1,
        slide(halo_bottom[3][0], -1),
        jnp.where(row == 0, slide(halo_bottom[1][0], 1), 0.0),
    )
    from_east, from_west = col_from_east[...], col_from_west[...]
    first = jnp.where(even, from_east, roll(from_west, 1))
    second = jnp.where(even, roll(from_east, -1), from_west)
    sign_ew = jnp.where(lane == COLS - 1, 1.0, -1.0)
    sign_ns = jnp.where(row == ROWS - 1, 1.0, -1.0)
    t_ew, s_ew = 0.08 * sign_ew, -0.06 * sign_ew
    t_ns, s_ns = 0.08 * sign_ns, -0.06 * sign_ns
    add_x, add_y = flow_x - mean_x, flow_y - mean_y
    upper = row < ROWS // 2

    def outer(k, carry):
        press_ew, press_ns = carry
        depth = lax.convert_element_type(k, f32)
        wet = centre > depth
        wet_ew, wet_ns = bottom_ew > depth, bottom_ns > depth
        sides = [
            pltpu.roll(source, (COLS - 1 - 2 * (k + base)) % COLS, 1)
            for source, base in ((first, 0), (first, 32), (second, 0), (second, 32))
        ]
        stacks = [
            jnp.where(
                upper,
                jnp.broadcast_to(row_south[pl.ds(i * LEVELS + k, 1), :], (ROWS, COLS)),
                jnp.broadcast_to(row_north[pl.ds(i * LEVELS + k, 1), :], (ROWS, COLS)),
            )
            for i in range(4)
        ]

        def lateral(i):
            cells = big[i, k]
            return jnp.where(wet_ew, sides[i] - cells, 0.0) + jnp.where(
                wet_ns, stacks[i] - cells, 0.0
            )

        press_ew = press_ew + jnp.where(wet_ew, t_ew * sides[2] + s_ew * sides[3], 0.0)
        press_ns = press_ns + jnp.where(wet_ns, t_ns * stacks[2] + s_ns * stacks[3], 0.0)
        x_out[k] = jnp.where(wet, x_out[k] + coef * lateral(0) + (press_ew + add_x), 0.0)
        y_out[k] = jnp.where(wet, y_out[k] + coef * lateral(1) + (press_ns + add_y), 0.0)
        t_out[k] = jnp.where(wet, t_out[k] + coef * lateral(2), 0.0)
        s_out[k] = jnp.where(wet, s_out[k] + coef * lateral(3), 0.0)
        return press_ew, press_ns

    lax.fori_loop(0, LEVELS, outer, (zero, zero), unroll=UNROLL)

    for copy in copies:
        copy.wait_send()


def body(*args):
    flat = jax.ShapeDtypeStruct((ROWS, COLS), f32)
    deep = jax.ShapeDtypeStruct((LEVELS, ROWS, COLS), f32)
    messages = len(OFFSETS) + 4
    return pl.pallas_call(
        kernel,
        out_shape=(flat,) * 3 + (deep,) * 4,
        in_specs=[pl.BlockSpec(memory_space=pl.ANY)] * 8,
        out_specs=(pl.BlockSpec(memory_space=pltpu.VMEM),) * 7,
        scratch_shapes=[
            pltpu.VMEM((ROWS, COLS), jnp.int32),
            pltpu.VMEM((4, ROWS, COLS), f32),
            pltpu.VMEM((4, LEVELS, ROWS, COLS), f32),
            pltpu.VMEM((ROWS, COLS), f32),
            pltpu.VMEM((len(SIDES), ROWS, COLS), f32),
            pltpu.VMEM((len(STACKS), 4, ROWS, COLS), f32),
            pltpu.VMEM((4 * LEVELS, COLS), f32),
            pltpu.VMEM((4 * LEVELS, COLS), f32),
            pltpu.VMEM((4 * LEVELS, COLS), f32),
            pltpu.VMEM((4 * LEVELS, COLS), f32),
            pltpu.VMEM((ROWS, COLS), f32),
            pltpu.VMEM((ROWS, COLS), f32),
            pltpu.VMEM((ROWS, COLS), f32),
            pltpu.VMEM((ROWS, COLS), f32),
            pltpu.SemaphoreType.DMA((8,)),
            pltpu.SemaphoreType.DMA((messages,)),
            pltpu.SemaphoreType.DMA((messages,)),
        ],
        compiler_params=pltpu.CompilerParams(
            collective_id=0, has_side_effects=True, vmem_limit_bytes=16 * 1024 * 1024
        ),
    )(*args)


def solution(mesh):
    flat, deep = P("lat", "lon"), P(None, "lat", "lon")
    return jax.shard_map(
        body,
        mesh=mesh,
        in_specs=(flat,) * 4 + (deep,) * 4,
        out_specs=(flat,) * 3 + (deep,) * 4,
        check_vma=False,
    )
```

```python
import jax
import jax.numpy as jnp
from jax import lax
from jax.experimental import pallas as pl
from jax.experimental.pallas import tpu as pltpu
from jax.sharding import PartitionSpec as P

LEVELS = 32
SUBCYCLES = 8
ROWS = 8
COLS = 128
EDGE = 16
WAVE = 0.45
CORIOLIS = 0.12
DIAPYCNAL = 0.2
UNROLL = 4

SIDES = [(a, o) for o in (-1, 1) for a in (-2, -1, 0, 1, 2)]
STACKS = [(a, 0) for a in (-2, -1, 1, 2)]
OFFSETS = SIDES + STACKS
f32 = jnp.float32


def kernel(
    bottom_hbm, level_hbm, flow_x_hbm, flow_y_hbm, x_hbm, y_hbm, t_hbm, s_hbm,
    flat_out, x_out, y_out, t_out, s_out,
    bottom, own, big, edge, side_recv, stack_recv,
    row_first, row_last, row_north, row_south,
    col_to_east, col_to_west, col_from_west, col_from_east,
    local_sem, send_sem, recv_sem,
):
    lat, lon = lax.axis_index("lat"), lax.axis_index("lon")
    lats, lons = lax.axis_size("lat"), lax.axis_size("lon")

    def place(offset):
        return {
            "lat": lax.rem(lat + offset[0] + lats, lats),
            "lon": lax.rem(lon + offset[1] + lons, lons),
        }

    barrier = pltpu.get_barrier_semaphore()
    for offset in OFFSETS:
        pl.semaphore_signal(
            barrier, inc=1, device_id=place(offset), device_id_type=pl.DeviceIdType.MESH
        )

    small = [
        pltpu.make_async_copy(bottom_hbm, bottom, local_sem.at[0]),
        pltpu.make_async_copy(level_hbm, own.at[1], local_sem.at[1]),
        pltpu.make_async_copy(flow_x_hbm, own.at[2], local_sem.at[2]),
        pltpu.make_async_copy(flow_y_hbm, own.at[3], local_sem.at[3]),
    ]
    large = [
        pltpu.make_async_copy(ref, big.at[i], local_sem.at[4 + i])
        for i, ref in enumerate((x_hbm, y_hbm, t_hbm, s_hbm))
    ]
    for copy in small + large:
        copy.start()

    lane = lax.broadcasted_iota(jnp.int32, (ROWS, COLS), 1)
    row = lax.broadcasted_iota(jnp.int32, (ROWS, COLS), 0)
    even = lane % 2 == 0

    def roll(cells, shift):
        return pltpu.roll(cells, shift % COLS, 1)

    def slide(cells, shift):
        return pltpu.roll(cells, shift % ROWS, 0)

    for copy in small:
        copy.wait()
    own[0] = bottom[...].astype(f32)
    packed = roll(own[0], EDGE)
    for i in range(1, 4):
        packed = jnp.where(lane // 32 == i, roll(own[i], EDGE + 32 * i), packed)
    edge[...] = packed

    pl.semaphore_wait(barrier, len(OFFSETS))

    copies = []

    def send(src, dst, index, offset):
        copy = pltpu.make_async_remote_copy(
            src_ref=src,
            dst_ref=dst,
            send_sem=send_sem.at[index],
            recv_sem=recv_sem.at[index],
            device_id=place(offset),
            device_id_type=pl.DeviceIdType.MESH,
        )
        copy.start()
        copies.append(copy)

    for a, o in SIDES:
        slot = SIDES.index((-a, -o))
        send(edge, side_recv.at[slot], slot, (a, o))
    for a, o in STACKS:
        slot = STACKS.index((-a, -o))
        send(own, stack_recv.at[slot], len(SIDES) + slot, (a, o))
    for copy in large:
        copy.wait()
    for i in range(4):
        row_first[pl.ds(i * LEVELS, LEVELS), :] = big[i, :, 0, :]
        row_last[pl.ds(i * LEVELS, LEVELS), :] = big[i, :, ROWS - 1, :]

    def pack(k, carry):
        first, second = carry
        first = jnp.where(lane // 2 == k, pltpu.roll(big[0, k], 2 * k + 1, 1), first)
        first = jnp.where(lane // 2 == k + 32, pltpu.roll(big[1, k], 2 * k + 65, 1), first)
        second = jnp.where(lane // 2 == k, pltpu.roll(big[2, k], 2 * k + 1, 1), second)
        second = jnp.where(
            lane // 2 == k + 32, pltpu.roll(big[3, k], (2 * k + 65) % COLS, 1), second
        )
        return first, second

    zero = jnp.zeros((ROWS, COLS), f32)
    first, second = lax.fori_loop(0, LEVELS, pack, (zero, zero), unroll=LEVELS)
    col_to_east[...] = jnp.where(even, first, roll(second, 1))
    col_to_west[...] = jnp.where(even, roll(first, -1), second)

    halo_count = len(OFFSETS)
    send(col_to_east, col_from_west, halo_count, (0, 1))
    send(col_to_west, col_from_east, halo_count + 1, (0, -1))
    send(row_last, row_south, halo_count + 2, (1, 0))
    send(row_first, row_north, halo_count + 3, (-1, 0))

    centre = own[0]
    coef = 0.08 + (0.12 / LEVELS) * centre
    bottom_e = jnp.where(lane == COLS - 1, 0.0, roll(centre, -1))
    bottom_w = jnp.where(lane == 0, 0.0, roll(centre, 1))
    bottom_n = jnp.where(row == ROWS - 1, 0.0, slide(centre, -1))
    bottom_s = jnp.where(row == 0, 0.0, slide(centre, 1))

    def inner(k, carry):
        press, sum_x, sum_y = carry
        depth = lax.convert_element_type(k, f32)
        wet = centre > depth
        wet_e, wet_w = bottom_e > depth, bottom_w > depth
        wet_n, wet_s = bottom_n > depth, bottom_s > depth

        def lateral(cells):
            return (
                jnp.where(wet_e, roll(cells, -1), cells)
                + jnp.where(wet_w, roll(cells, 1), cells)
                + jnp.where(wet_n, slide(cells, -1), cells)
                + jnp.where(wet_s, slide(cells, 1), cells)
                - 4.0 * cells
            )

        x, y, t, s = big[0, k], big[1, k], big[2, k], big[3, k]
        press = press + jnp.where(wet, 0.6 * s - 0.8 * t, 0.0)
        press_x = jnp.where(lane == COLS - 1, 0.0, roll(press, -1)) - jnp.where(
            lane == 0, 0.0, roll(press, 1)
        )
        press_y = jnp.where(row == ROWS - 1, 0.0, slide(press, -1)) - jnp.where(
            row == 0, 0.0, slide(press, 1)
        )
        x_out[k] = x + coef * lateral(x) + CORIOLIS * y - 0.1 * press_x
        y_out[k] = y + coef * lateral(y) - CORIOLIS * x - 0.1 * press_y
        below = centre > depth + 1.0
        up, down = lax.max(k - 1, 0), lax.min(k + 1, LEVELS - 1)
        for i, cells, out in ((2, t, t_out), (3, s, s_out)):
            vertical = (big[i, up] - cells) + jnp.where(below, big[i, down] - cells, 0.0)
            out[k] = cells + coef * lateral(cells) + DIAPYCNAL * vertical
        return press, sum_x + jnp.where(wet, x, 0.0), sum_y + jnp.where(wet, y, 0.0)

    _, sum_x, sum_y = lax.fori_loop(0, LEVELS, inner, (zero, zero, zero), unroll=UNROLL)
    count = jnp.maximum(centre, 1.0)
    mean_x, mean_y = sum_x / count, sum_y / count

    for copy in copies[:halo_count]:
        copy.wait_recv()

    fields = [[], [], [], []]
    for a in (-2, -1, 0, 1, 2):
        inside = (lat + a >= 0) & (lat + a < lats)
        keep = jnp.where(inside, 1.0, 0.0).astype(f32)
        merged = jnp.where(
            lane % 32 < EDGE, side_recv[SIDES.index((a, -1))], side_recv[SIDES.index((a, 1))]
        )
        for i in range(4):
            middle = own[i] if a == 0 else stack_recv[STACKS.index((a, 0)), i]
            beside = roll(merged, -(EDGE + 32 * i))
            if i == 0 and a != 0:
                middle, beside = middle * keep, beside * keep
            fields[i].append((middle, beside))
    halo_bottom = fields[0]

    def whole(tiles):
        return jnp.concatenate(
            [jnp.concatenate([m for m, _ in tiles], 0), jnp.concatenate([b for _, b in tiles], 0)], 1
        )

    def ew(cells):
        return pltpu.roll(cells, 2 * COLS - 1, 1) - pltpu.roll(cells, 1, 1)

    def ns(cells):
        return pltpu.roll(cells, cells.shape[0] - 1, 0) - pltpu.roll(cells, 1, 0)

    column, level, flow_x, flow_y = (whole(tiles) for tiles in fields)
    wet = jnp.where(column > 0.0, 1.0, 0.0)
    gain = (WAVE / LEVELS) * column
    level, flow_x, flow_y = wet * level, wet * flow_x, wet * flow_y
    for cycle in range(SUBCYCLES):
        level = level - wet * (ew(gain * flow_x) + ns(gain * flow_y))
        flow_x, flow_y = (
            flow_x - gain * ew(level) + CORIOLIS * flow_y,
            flow_y - gain * ns(level) - CORIOLIS * flow_x,
        )
        if cycle == 3:
            wet, gain, level, flow_x, flow_y = (
                cells[ROWS : 4 * ROWS] for cells in (wet, gain, level, flow_x, flow_y)
            )
    level, flow_x, flow_y = (cells[ROWS : 2 * ROWS, :COLS] for cells in (level, flow_x, flow_y))
    flat_out[0] = level
    flat_out[1] = flow_x
    flat_out[2] = flow_y

    for copy in copies[halo_count:]:
        copy.wait_recv()

    beside = halo_bottom[2][1]
    bottom_ew = jnp.where(
        lane == COLS - 1, roll(beside, -1), jnp.where(lane == 0, roll(beside, 1), 0.0)
    )
    bottom_ns = jnp.where(
        row == ROWS - 1,
        slide(halo_bottom[3][0], -1),
        jnp.where(row == 0, slide(halo_bottom[1][0], 1), 0.0),
    )
    from_east, from_west = col_from_east[...], col_from_west[...]
    first = jnp.where(even, from_east, roll(from_west, 1))
    second = jnp.where(even, roll(from_east, -1), from_west)
    sign_ew = jnp.where(lane == COLS - 1, 1.0, -1.0)
    sign_ns = jnp.where(row == ROWS - 1, 1.0, -1.0)
    t_ew, s_ew = 0.08 * sign_ew, -0.06 * sign_ew
    t_ns, s_ns = 0.08 * sign_ns, -0.06 * sign_ns
    add_x, add_y = flow_x - mean_x, flow_y - mean_y
    upper = row < ROWS // 2

    def outer(k, carry):
        press_ew, press_ns = carry
        depth = lax.convert_element_type(k, f32)
        wet = centre > depth
        wet_ew, wet_ns = bottom_ew > depth, bottom_ns > depth
        sides = [
            pltpu.roll(source, (COLS - 1 - 2 * (k + base)) % COLS, 1)
            for source, base in ((first, 0), (first, 32), (second, 0), (second, 32))
        ]
        stacks = [
            jnp.where(
                upper,
                jnp.broadcast_to(row_south[pl.ds(i * LEVELS + k, 1), :], (ROWS, COLS)),
                jnp.broadcast_to(row_north[pl.ds(i * LEVELS + k, 1), :], (ROWS, COLS)),
            )
            for i in range(4)
        ]

        def lateral(i):
            cells = big[i, k]
            return jnp.where(wet_ew, sides[i] - cells, 0.0) + jnp.where(
                wet_ns, stacks[i] - cells, 0.0
            )

        press_ew = press_ew + jnp.where(wet_ew, t_ew * sides[2] + s_ew * sides[3], 0.0)
        press_ns = press_ns + jnp.where(wet_ns, t_ns * stacks[2] + s_ns * stacks[3], 0.0)
        x_out[k] = jnp.where(wet, x_out[k] + coef * lateral(0) + (press_ew + add_x), 0.0)
        y_out[k] = jnp.where(wet, y_out[k] + coef * lateral(1) + (press_ns + add_y), 0.0)
        t_out[k] = jnp.where(wet, t_out[k] + coef * lateral(2), 0.0)
        s_out[k] = jnp.where(wet, s_out[k] + coef * lateral(3), 0.0)
        return press_ew, press_ns

    lax.fori_loop(0, LEVELS, outer, (zero, zero), unroll=UNROLL)

    for copy in copies:
        copy.wait_send()


def store(flat, x, y, t, s, *rest):
    outs, sem = rest[:-1], rest[-1]
    sources = [flat.at[i] for i in range(3)] + [x, y, t, s]
    copies = [
        pltpu.make_async_copy(source, out, sem.at[i])
        for i, (source, out) in enumerate(zip(sources, outs))
    ]
    for copy in copies:
        copy.start()
    for copy in copies:
        copy.wait()


def body(*args):
    flat = jax.ShapeDtypeStruct((ROWS, COLS), f32)
    deep = jax.ShapeDtypeStruct((LEVELS, ROWS, COLS), f32)
    messages = len(OFFSETS) + 4
    args = [pltpu.with_memory_space_constraint(arg, pltpu.HBM) for arg in args]
    held = pl.pallas_call(
        kernel,
        out_shape=(pltpu.VMEM((3, ROWS, COLS), f32),)
        + (pltpu.VMEM((LEVELS, ROWS, COLS), f32),) * 4,
        in_specs=[pl.BlockSpec(memory_space=pltpu.HBM)] * 8,
        out_specs=(pl.BlockSpec(memory_space=pltpu.VMEM),) * 5,
        scratch_shapes=[
            pltpu.VMEM((ROWS, COLS), jnp.int32),
            pltpu.VMEM((4, ROWS, COLS), f32),
            pltpu.VMEM((4, LEVELS, ROWS, COLS), f32),
            pltpu.VMEM((ROWS, COLS), f32),
            pltpu.VMEM((len(SIDES), ROWS, COLS), f32),
            pltpu.VMEM((len(STACKS), 4, ROWS, COLS), f32),
            pltpu.VMEM((4 * LEVELS, COLS), f32),
            pltpu.VMEM((4 * LEVELS, COLS), f32),
            pltpu.VMEM((4 * LEVELS, COLS), f32),
            pltpu.VMEM((4 * LEVELS, COLS), f32),
            pltpu.VMEM((ROWS, COLS), f32),
            pltpu.VMEM((ROWS, COLS), f32),
            pltpu.VMEM((ROWS, COLS), f32),
            pltpu.VMEM((ROWS, COLS), f32),
            pltpu.SemaphoreType.DMA((8,)),
            pltpu.SemaphoreType.DMA((messages,)),
            pltpu.SemaphoreType.DMA((messages,)),
        ],
        compiler_params=pltpu.CompilerParams(
            collective_id=0, has_side_effects=True, vmem_limit_bytes=16 * 1024 * 1024
        ),
        name="step",
    )(*args)
    return pl.pallas_call(
        store,
        out_shape=(flat,) * 3 + (deep,) * 4,
        in_specs=[pl.BlockSpec(memory_space=pltpu.VMEM)] * 5,
        out_specs=(pl.BlockSpec(memory_space=pltpu.HBM),) * 7,
        scratch_shapes=[pltpu.SemaphoreType.DMA((7,))],
        name="store",
    )(*held)


def solution(mesh):
    flat, deep = P("lat", "lon"), P(None, "lat", "lon")
    return jax.shard_map(
        body,
        mesh=mesh,
        in_specs=(flat,) * 4 + (deep,) * 4,
        out_specs=(flat,) * 3 + (deep,) * 4,
        check_vma=False,
    )
```

```python
import jax
import jax.numpy as jnp
from jax import lax
from jax.experimental import pallas as pl
from jax.experimental.pallas import tpu as pltpu
from jax.sharding import PartitionSpec as P

LEVELS = 32
SUBCYCLES = 8
ROWS = 8
COLS = 128
EDGE = 16
WAVE = 0.45
CORIOLIS = 0.12
DIAPYCNAL = 0.2

LATS = (-2, -1, 0, 1, 2)
OFFSETS = (
    (0, 1), (1, 0), (1, 1), (2, 0), (2, 1),
    (-1, 0), (-1, 1), (-2, 0), (-2, 1),
    (0, -1), (1, -1), (2, -1), (-1, -1), (-2, -1),
)
f32 = jnp.float32


def kernel(
    bottom_hbm, level_hbm, flow_x_hbm, flow_y_hbm, x_hbm, y_hbm, t_hbm, s_hbm,
    flat_out, x_out, y_out, t_out, s_out,
    bottom, own, big, edge, side_recv, stack_recv,
    rows_send, rows_recv, cols_send, cols_recv,
    local_sem, send_sem, recv_sem,
):
    lat, lon = lax.axis_index("lat"), lax.axis_index("lon")
    lats, lons = lax.axis_size("lat"), lax.axis_size("lon")

    def flag(condition):
        return jnp.where(condition, 1, 0)

    spot, core = lax.rem(lat, 8), lax.rem(lon, 2)
    within = lax.rem(lon, 8)
    seam = flag(within == 0) + flag(within == 7)
    western = lax.rem(lax.div(lon, 8) + 3 + core, 4)
    up, across = 1 - 2 * flag(spot >= 4), 1 - 2 * core

    def roles(a_sign, o_sign):
        a, o = a_sign * up, o_sign * across
        if o_sign == 0:
            lead = flag(spot < lax.rem(lat + a + lats, 8))
            return a, o, lead, 1 - lead
        if o_sign == 1:
            return a, o, core, 1 - core
        far = core * flag(spot + a < 0) + (1 - core) * flag(spot + a >= 8)
        west = flag(western == 0) + flag(western == 1) * (1 - far)
        east = flag(western == 3)
        lead = core * west + (1 - core) * east
        trail = core * east + (1 - core) * west
        return a, o, seam * lead + (1 - seam) * core, seam * trail + (1 - seam) * (1 - core)

    neighbours = [(sign, *roles(*sign)) for sign in OFFSETS]

    def place(a, o):
        return {"lat": lax.rem(lat + a + lats, lats), "lon": lax.rem(lon + o + lons, lons)}

    barrier = pltpu.get_barrier_semaphore()
    for _, a, o, _, trail in neighbours[::-1]:

        @pl.when(trail == 0)
        def _(a=a, o=o):
            pl.semaphore_signal(
                barrier, inc=1, device_id=place(a, o), device_id_type=pl.DeviceIdType.MESH
            )

    awaited = sum(1 - lead for _, _, _, lead, _ in neighbours)

    small = [
        pltpu.make_async_copy(bottom_hbm, bottom, local_sem.at[0]),
        pltpu.make_async_copy(level_hbm, own.at[1], local_sem.at[1]),
        pltpu.make_async_copy(flow_x_hbm, own.at[2], local_sem.at[2]),
        pltpu.make_async_copy(flow_y_hbm, own.at[3], local_sem.at[3]),
    ]
    large = [
        pltpu.make_async_copy(ref, big.at[i], local_sem.at[4 + i])
        for i, ref in enumerate((x_hbm, y_hbm, t_hbm, s_hbm))
    ]
    for copy in small + large:
        copy.start()

    lane = lax.broadcasted_iota(jnp.int32, (ROWS, COLS), 1)
    row = lax.broadcasted_iota(jnp.int32, (ROWS, COLS), 0)
    even = lane % 2 == 0

    def roll(cells, shift):
        return pltpu.roll(cells, shift % COLS, 1)

    def slide(cells, shift):
        return pltpu.roll(cells, shift % ROWS, 0)

    for copy in small:
        copy.wait()
    own[0] = bottom[...].astype(f32)
    packed = roll(own[0], EDGE)
    for i in range(1, 4):
        packed = jnp.where(lane // 32 == i, roll(own[i], EDGE + 32 * i), packed)
    edge[...] = packed

    def message(src, dst, index, a, o):
        return pltpu.make_async_remote_copy(
            src_ref=src,
            dst_ref=dst,
            send_sem=send_sem.at[index],
            recv_sem=recv_sem.at[index],
            device_id=place(a, o),
            device_id_type=pl.DeviceIdType.MESH,
        )

    def halo(sign, a, o):
        if sign[1] == 0:
            return message(own, stack_recv.at[2 - a], 12 - a, a, o)
        slot = 2 - a + 5 * lax.div(1 - o, 2)
        return message(edge, side_recv.at[slot], slot, a, o)

    def deep_edge(sign, a, o):
        if sign[1] == 0:
            there, slot = lax.div(a + 1, 2), lax.div(1 - a, 2)
            return message(rows_send.at[there], rows_recv.at[slot], 15 + slot, a, o)
        there, slot = lax.div(o + 1, 2), lax.div(1 - o, 2)
        return message(cols_send.at[there], cols_recv.at[slot], 17 + slot, a, o)

    def adjacent(sign):
        return abs(sign[0]) + abs(sign[1]) == 1

    @pl.when(awaited > 0)
    def _():
        pl.semaphore_wait(barrier, awaited)

    for sign, a, o, lead, _ in neighbours[::-1]:

        @pl.when(lead == 0)
        def _(sign=sign, a=a, o=o):
            halo(sign, a, o).start()

    for copy in large:
        copy.wait()
    for i in range(4):
        rows_send[0, pl.ds(i * LEVELS, LEVELS), :] = big[i, :, 0, :]
        rows_send[1, pl.ds(i * LEVELS, LEVELS), :] = big[i, :, ROWS - 1, :]

    def pack(k, carry):
        first, second = carry
        first = jnp.where(lane // 2 == k, pltpu.roll(big[0, k], 2 * k + 1, 1), first)
        first = jnp.where(lane // 2 == k + 32, pltpu.roll(big[1, k], 2 * k + 65, 1), first)
        second = jnp.where(lane // 2 == k, pltpu.roll(big[2, k], 2 * k + 1, 1), second)
        second = jnp.where(
            lane // 2 == k + 32, pltpu.roll(big[3, k], (2 * k + 65) % COLS, 1), second
        )
        return first, second

    zero = jnp.zeros((ROWS, COLS), f32)
    first, second = lax.fori_loop(0, LEVELS, pack, (zero, zero), unroll=LEVELS)
    cols_send[1] = jnp.where(even, first, roll(second, 1))
    cols_send[0] = jnp.where(even, roll(first, -1), second)

    for sign, a, o, lead, _ in neighbours:
        if adjacent(sign):

            @pl.when(lead == 0)
            def _(sign=sign, a=a, o=o):
                deep_edge(sign, a, o).start()

    centre = own[0]
    coef = 0.08 + (0.12 / LEVELS) * centre
    bottom_e = jnp.where(lane == COLS - 1, 0.0, roll(centre, -1))
    bottom_w = jnp.where(lane == 0, 0.0, roll(centre, 1))
    bottom_n = jnp.where(row == ROWS - 1, 0.0, slide(centre, -1))
    bottom_s = jnp.where(row == 0, 0.0, slide(centre, 1))

    def inner(k, carry):
        press, sum_x, sum_y = carry
        depth = lax.convert_element_type(k, f32)
        wet = centre > depth
        wet_e, wet_w = bottom_e > depth, bottom_w > depth
        wet_n, wet_s = bottom_n > depth, bottom_s > depth

        def lateral(cells):
            return (
                jnp.where(wet_e, roll(cells, -1), cells)
                + jnp.where(wet_w, roll(cells, 1), cells)
                + jnp.where(wet_n, slide(cells, -1), cells)
                + jnp.where(wet_s, slide(cells, 1), cells)
                - 4.0 * cells
            )

        x, y, t, s = big[0, k], big[1, k], big[2, k], big[3, k]
        press = press + jnp.where(wet, 0.6 * s - 0.8 * t, 0.0)
        press_x = jnp.where(lane == COLS - 1, 0.0, roll(press, -1)) - jnp.where(
            lane == 0, 0.0, roll(press, 1)
        )
        press_y = jnp.where(row == ROWS - 1, 0.0, slide(press, -1)) - jnp.where(
            row == 0, 0.0, slide(press, 1)
        )
        x_out[k] = x + coef * lateral(x) + CORIOLIS * y - 0.1 * press_x
        y_out[k] = y + coef * lateral(y) - CORIOLIS * x - 0.1 * press_y
        below = centre > depth + 1.0
        up, down = lax.max(k - 1, 0), lax.min(k + 1, LEVELS - 1)
        for i, cells, out in ((2, t, t_out), (3, s, s_out)):
            vertical = (big[i, up] - cells) + jnp.where(below, big[i, down] - cells, 0.0)
            out[k] = cells + coef * lateral(cells) + DIAPYCNAL * vertical
        return press, sum_x + jnp.where(wet, x, 0.0), sum_y + jnp.where(wet, y, 0.0)

    _, sum_x, sum_y = lax.fori_loop(0, LEVELS, inner, (zero, zero, zero), unroll=LEVELS)
    count = jnp.maximum(centre, 1.0)
    mean_x, mean_y = sum_x / count, sum_y / count

    for sign, a, o, lead, _ in neighbours:

        @pl.when(lead == 1)
        def _(sign=sign, a=a, o=o):
            halo(sign, -a, -o).wait_recv()
            halo(sign, a, o).start()
            if adjacent(sign):
                deep_edge(sign, a, o).start()

    for sign, a, o, lead, _ in neighbours:

        @pl.when(lead == 0)
        def _(sign=sign, a=a, o=o):
            halo(sign, -a, -o).wait_recv()

    fields = [[], [], [], []]
    for a in (-2, -1, 0, 1, 2):
        inside = (lat + a >= 0) & (lat + a < lats)
        keep = jnp.where(inside, 1.0, 0.0).astype(f32)
        merged = jnp.where(lane % 32 < EDGE, side_recv[a + 2], side_recv[a + 7])
        for i in range(4):
            middle = own[i] if a == 0 else stack_recv[a + 2, i]
            beside = roll(merged, -(EDGE + 32 * i))
            if i == 0 and a != 0:
                middle, beside = middle * keep, beside * keep
            fields[i].append((middle, beside))
    halo_bottom = fields[0]

    def whole(tiles):
        return jnp.concatenate(
            [jnp.concatenate([m for m, _ in tiles], 0), jnp.concatenate([b for _, b in tiles], 0)], 1
        )

    def ew(cells):
        return pltpu.roll(cells, 2 * COLS - 1, 1) - pltpu.roll(cells, 1, 1)

    def ns(cells):
        return pltpu.roll(cells, cells.shape[0] - 1, 0) - pltpu.roll(cells, 1, 0)

    column, level, flow_x, flow_y = (whole(tiles) for tiles in fields)
    wet = jnp.where(column > 0.0, 1.0, 0.0)
    gain = (WAVE / LEVELS) * column
    level, flow_x, flow_y = wet * level, wet * flow_x, wet * flow_y
    for cycle in range(SUBCYCLES):
        level = level - wet * (ew(gain * flow_x) + ns(gain * flow_y))
        flow_x, flow_y = (
            flow_x - gain * ew(level) + CORIOLIS * flow_y,
            flow_y - gain * ns(level) - CORIOLIS * flow_x,
        )
        if cycle == 3:
            wet, gain, level, flow_x, flow_y = (
                cells[ROWS : 4 * ROWS] for cells in (wet, gain, level, flow_x, flow_y)
            )
    level, flow_x, flow_y = (cells[ROWS : 2 * ROWS, :COLS] for cells in (level, flow_x, flow_y))
    flat_out[0] = level
    flat_out[1] = flow_x
    flat_out[2] = flow_y

    for sign, a, o, _, _ in neighbours:
        if adjacent(sign):
            deep_edge(sign, -a, -o).wait_recv()

    beside = halo_bottom[2][1]
    bottom_ew = jnp.where(
        lane == COLS - 1, roll(beside, -1), jnp.where(lane == 0, roll(beside, 1), 0.0)
    )
    bottom_ns = jnp.where(
        row == ROWS - 1,
        slide(halo_bottom[3][0], -1),
        jnp.where(row == 0, slide(halo_bottom[1][0], 1), 0.0),
    )
    from_west, from_east = cols_recv[0], cols_recv[1]
    first = jnp.where(even, from_east, roll(from_west, 1))
    second = jnp.where(even, roll(from_east, -1), from_west)
    sign_ew = jnp.where(lane == COLS - 1, 1.0, -1.0)
    sign_ns = jnp.where(row == ROWS - 1, 1.0, -1.0)
    t_ew, s_ew = 0.08 * sign_ew, -0.06 * sign_ew
    t_ns, s_ns = 0.08 * sign_ns, -0.06 * sign_ns
    add_x, add_y = flow_x - mean_x, flow_y - mean_y
    upper = row < ROWS // 2

    def outer(k, carry):
        press_ew, press_ns = carry
        depth = lax.convert_element_type(k, f32)
        wet = centre > depth
        wet_ew, wet_ns = bottom_ew > depth, bottom_ns > depth
        sides = [
            pltpu.roll(source, (COLS - 1 - 2 * (k + base)) % COLS, 1)
            for source, base in ((first, 0), (first, 32), (second, 0), (second, 32))
        ]
        stacks = [
            jnp.where(
                upper,
                jnp.broadcast_to(rows_recv[0, pl.ds(i * LEVELS + k, 1), :], (ROWS, COLS)),
                jnp.broadcast_to(rows_recv[1, pl.ds(i * LEVELS + k, 1), :], (ROWS, COLS)),
            )
            for i in range(4)
        ]

        def lateral(i):
            cells = big[i, k]
            return jnp.where(wet_ew, sides[i] - cells, 0.0) + jnp.where(
                wet_ns, stacks[i] - cells, 0.0
            )

        press_ew = press_ew + jnp.where(wet_ew, t_ew * sides[2] + s_ew * sides[3], 0.0)
        press_ns = press_ns + jnp.where(wet_ns, t_ns * stacks[2] + s_ns * stacks[3], 0.0)
        x_out[k] = jnp.where(wet, x_out[k] + coef * lateral(0) + (press_ew + add_x), 0.0)
        y_out[k] = jnp.where(wet, y_out[k] + coef * lateral(1) + (press_ns + add_y), 0.0)
        t_out[k] = jnp.where(wet, t_out[k] + coef * lateral(2), 0.0)
        s_out[k] = jnp.where(wet, s_out[k] + coef * lateral(3), 0.0)
        return press_ew, press_ns

    lax.fori_loop(0, LEVELS, outer, (zero, zero), unroll=LEVELS)

    for sign, a, o, _, _ in neighbours:
        halo(sign, a, o).wait_send()
        if adjacent(sign):
            deep_edge(sign, a, o).wait_send()


def store(flat, x, y, t, s, *rest):
    outs, sem = rest[:-1], rest[-1]
    sources = [flat.at[i] for i in range(3)] + [x, y, t, s]
    copies = [
        pltpu.make_async_copy(source, out, sem.at[i])
        for i, (source, out) in enumerate(zip(sources, outs))
    ]
    for copy in copies:
        copy.start()
    for copy in copies:
        copy.wait()


def body(*args):
    flat = jax.ShapeDtypeStruct((ROWS, COLS), f32)
    deep = jax.ShapeDtypeStruct((LEVELS, ROWS, COLS), f32)
    messages = 19
    args = [pltpu.with_memory_space_constraint(arg, pltpu.HBM) for arg in args]
    held = pl.pallas_call(
        kernel,
        out_shape=(pltpu.VMEM((3, ROWS, COLS), f32),)
        + (pltpu.VMEM((LEVELS, ROWS, COLS), f32),) * 4,
        in_specs=[pl.BlockSpec(memory_space=pltpu.HBM)] * 8,
        out_specs=(pl.BlockSpec(memory_space=pltpu.VMEM),) * 5,
        scratch_shapes=[
            pltpu.VMEM((ROWS, COLS), jnp.int32),
            pltpu.VMEM((4, ROWS, COLS), f32),
            pltpu.VMEM((4, LEVELS, ROWS, COLS), f32),
            pltpu.VMEM((ROWS, COLS), f32),
            pltpu.VMEM((10, ROWS, COLS), f32),
            pltpu.VMEM((5, 4, ROWS, COLS), f32),
            pltpu.VMEM((2, 4 * LEVELS, COLS), f32),
            pltpu.VMEM((2, 4 * LEVELS, COLS), f32),
            pltpu.VMEM((2, ROWS, COLS), f32),
            pltpu.VMEM((2, ROWS, COLS), f32),
            pltpu.SemaphoreType.DMA((8,)),
            pltpu.SemaphoreType.DMA((messages,)),
            pltpu.SemaphoreType.DMA((messages,)),
        ],
        compiler_params=pltpu.CompilerParams(
            collective_id=0, has_side_effects=True, vmem_limit_bytes=16 * 1024 * 1024
        ),
        name="step",
    )(*args)
    return pl.pallas_call(
        store,
        out_shape=(flat,) * 3 + (deep,) * 4,
        in_specs=[pl.BlockSpec(memory_space=pltpu.VMEM)] * 5,
        out_specs=(pl.BlockSpec(memory_space=pltpu.HBM),) * 7,
        scratch_shapes=[pltpu.SemaphoreType.DMA((7,))],
        compiler_params=pltpu.CompilerParams(vmem_limit_bytes=1024 * 1024),
        name="store",
    )(*(pltpu.with_memory_space_constraint(cells, pltpu.VMEM) for cells in held))


def solution(mesh):
    flat, deep = P("lat", "lon"), P(None, "lat", "lon")
    return jax.shard_map(
        body,
        mesh=mesh,
        in_specs=(flat,) * 4 + (deep,) * 4,
        out_specs=(flat,) * 3 + (deep,) * 4,
        check_vma=False,
    )
```

```python
import jax
import jax.numpy as jnp
from jax import lax
from jax.experimental import pallas as pl
from jax.experimental.pallas import tpu as pltpu
from jax.sharding import PartitionSpec as P

LEVELS = 32
SUBCYCLES = 8
ROWS = 8
COLS = 128
EDGE = 16
WAVE = 0.45
CORIOLIS = 0.12
DIAPYCNAL = 0.2

LATS = (-2, -1, 0, 1, 2)
OFFSETS = (
    (0, 1), (1, 0), (1, 1), (2, 0), (2, 1),
    (-1, 0), (-1, 1), (-2, 0), (-2, 1),
    (0, -1), (1, -1), (2, -1), (-1, -1), (-2, -1),
)
f32 = jnp.float32


def kernel(
    bottom_hbm, level_hbm, flow_x_hbm, flow_y_hbm, x_hbm, y_hbm, t_hbm, s_hbm,
    flat_out, x_out, y_out, t_out, s_out,
    bottom, own, big, edge, side_recv, stack_recv,
    rows_send, rows_recv, cols_send, cols_recv,
    local_sem, send_sem, recv_sem,
):
    lat, lon = lax.axis_index("lat"), lax.axis_index("lon")
    lats, lons = lax.axis_size("lat"), lax.axis_size("lon")

    small = [
        pltpu.make_async_copy(bottom_hbm, bottom, local_sem.at[0]),
        pltpu.make_async_copy(level_hbm, own.at[1], local_sem.at[1]),
        pltpu.make_async_copy(flow_x_hbm, own.at[2], local_sem.at[2]),
        pltpu.make_async_copy(flow_y_hbm, own.at[3], local_sem.at[3]),
    ]
    large = [
        pltpu.make_async_copy(ref, big.at[i], local_sem.at[4 + i])
        for i, ref in enumerate((x_hbm, y_hbm, t_hbm, s_hbm))
    ]
    for copy in small + large:
        copy.start()

    def flag(condition):
        return jnp.where(condition, 1, 0)

    spot, core = lax.rem(lat, 8), lax.rem(lon, 2)
    within = lax.rem(lon, 8)
    seam = flag(within == 0) + flag(within == 7)
    western = lax.rem(lax.div(lon, 8) + 3 + core, 4)
    up, across = 1 - 2 * flag(spot >= 4), 1 - 2 * core

    def roles(a_sign, o_sign):
        a, o = a_sign * up, o_sign * across
        if o_sign == 0:
            lead = flag(spot < lax.rem(lat + a + lats, 8))
            return a, o, lead, 1 - lead
        beyond = flag(spot + a < 0) + flag(spot + a >= 8)
        near = jnp.where(
            beyond == 0,
            core,
            jnp.where(lax.div(lon, 8) == 3, flag(o < 0), flag(spot < lax.rem(lat + a + lats, 8))),
        )
        if o_sign == 1:
            return a, o, near, 1 - near
        far = core * flag(spot + a < 0) + (1 - core) * flag(spot + a >= 8)
        west = flag(western == 0) + flag(western == 1) * (1 - far)
        east = flag(western == 3)
        lead = core * west + (1 - core) * east
        trail = core * east + (1 - core) * west
        return a, o, jnp.where(seam == 1, lead, near), jnp.where(seam == 1, trail, 1 - near)

    def is_first(a, o):
        return flag(lax.rem(lat + a + lats, lats) + lax.rem(lon + o + lons, lons) == 0)

    def settled(a_sign, o_sign):
        a, o, lead, trail = roles(a_sign, o_sign)
        if o_sign != -1:
            lead = jnp.where(is_first(0, 0) == 1, 0, lead)
            trail = jnp.where(is_first(0, 0) == 1, 1, trail)
        first = is_first(a, o) * flag(o != 1)
        return a, o, jnp.where(first == 1, 1, lead), jnp.where(first == 1, 0, trail)

    neighbours = [(sign, *settled(*sign)) for sign in OFFSETS]

    def place(a, o):
        return {"lat": lax.rem(lat + a + lats, lats), "lon": lax.rem(lon + o + lons, lons)}

    barrier = pltpu.get_barrier_semaphore()
    for _, a, o, _, trail in neighbours[::-1]:

        @pl.when(trail == 0)
        def _(a=a, o=o):
            pl.semaphore_signal(
                barrier, inc=1, device_id=place(a, o), device_id_type=pl.DeviceIdType.MESH
            )

    awaited = sum(1 - lead for _, _, _, lead, _ in neighbours)

    lane = lax.broadcasted_iota(jnp.int32, (ROWS, COLS), 1)
    row = lax.broadcasted_iota(jnp.int32, (ROWS, COLS), 0)
    even = lane % 2 == 0

    def roll(cells, shift):
        return pltpu.roll(cells, shift % COLS, 1)

    def slide(cells, shift):
        return pltpu.roll(cells, shift % ROWS, 0)

    for copy in small:
        copy.wait()
    own[0] = bottom[...].astype(f32)
    packed = roll(own[0], EDGE)
    for i in range(1, 4):
        packed = jnp.where(lane // 32 == i, roll(own[i], EDGE + 32 * i), packed)
    edge[...] = packed

    def message(src, dst, index, a, o):
        return pltpu.make_async_remote_copy(
            src_ref=src,
            dst_ref=dst,
            send_sem=send_sem.at[index],
            recv_sem=recv_sem.at[index],
            device_id=place(a, o),
            device_id_type=pl.DeviceIdType.MESH,
        )

    def halo(sign, a, o):
        if sign[1] == 0:
            return message(own, stack_recv.at[2 - a], 12 - a, a, o)
        slot = 2 - a + 5 * lax.div(1 - o, 2)
        return message(edge, side_recv.at[slot], slot, a, o)

    def deep_edge(sign, a, o):
        if sign[1] == 0:
            there, slot = lax.div(a + 1, 2), lax.div(1 - a, 2)
            return message(rows_send.at[there], rows_recv.at[slot], 15 + slot, a, o)
        there, slot = lax.div(o + 1, 2), lax.div(1 - o, 2)
        return message(cols_send.at[there], cols_recv.at[slot], 17 + slot, a, o)

    def adjacent(sign):
        return abs(sign[0]) + abs(sign[1]) == 1

    @pl.when(awaited > 0)
    def _():
        pl.semaphore_wait(barrier, awaited)

    for sign, a, o, lead, _ in neighbours[::-1]:

        @pl.when(lead == 0)
        def _(sign=sign, a=a, o=o):
            halo(sign, a, o).start()

    for copy in large:
        copy.wait()
    for i in range(4):
        rows_send[0, pl.ds(i * LEVELS, LEVELS), :] = big[i, :, 0, :]
        rows_send[1, pl.ds(i * LEVELS, LEVELS), :] = big[i, :, ROWS - 1, :]

    def pack(k, carry):
        first, second = carry
        first = jnp.where(lane // 2 == k, pltpu.roll(big[0, k], 2 * k + 1, 1), first)
        first = jnp.where(lane // 2 == k + 32, pltpu.roll(big[1, k], 2 * k + 65, 1), first)
        second = jnp.where(lane // 2 == k, pltpu.roll(big[2, k], 2 * k + 1, 1), second)
        second = jnp.where(
            lane // 2 == k + 32, pltpu.roll(big[3, k], (2 * k + 65) % COLS, 1), second
        )
        return first, second

    zero = jnp.zeros((ROWS, COLS), f32)
    first, second = lax.fori_loop(0, LEVELS, pack, (zero, zero), unroll=LEVELS)
    cols_send[1] = jnp.where(even, first, roll(second, 1))
    cols_send[0] = jnp.where(even, roll(first, -1), second)

    for sign, a, o, lead, _ in neighbours:
        if adjacent(sign):

            @pl.when(lead == 0)
            def _(sign=sign, a=a, o=o):
                deep_edge(sign, a, o).start()

    centre = own[0]
    coef = 0.08 + (0.12 / LEVELS) * centre
    bottom_e = jnp.where(lane == COLS - 1, 0.0, roll(centre, -1))
    bottom_w = jnp.where(lane == 0, 0.0, roll(centre, 1))
    bottom_n = jnp.where(row == ROWS - 1, 0.0, slide(centre, -1))
    bottom_s = jnp.where(row == 0, 0.0, slide(centre, 1))

    def inner(k, carry):
        press, sum_x, sum_y = carry
        depth = lax.convert_element_type(k, f32)
        wet = centre > depth
        wet_e, wet_w = bottom_e > depth, bottom_w > depth
        wet_n, wet_s = bottom_n > depth, bottom_s > depth

        def lateral(cells):
            return (
                jnp.where(wet_e, roll(cells, -1), cells)
                + jnp.where(wet_w, roll(cells, 1), cells)
                + jnp.where(wet_n, slide(cells, -1), cells)
                + jnp.where(wet_s, slide(cells, 1), cells)
                - 4.0 * cells
            )

        x, y, t, s = big[0, k], big[1, k], big[2, k], big[3, k]
        press = press + jnp.where(wet, 0.6 * s - 0.8 * t, 0.0)
        press_x = jnp.where(lane == COLS - 1, 0.0, roll(press, -1)) - jnp.where(
            lane == 0, 0.0, roll(press, 1)
        )
        press_y = jnp.where(row == ROWS - 1, 0.0, slide(press, -1)) - jnp.where(
            row == 0, 0.0, slide(press, 1)
        )
        x_out[k] = x + coef * lateral(x) + CORIOLIS * y - 0.1 * press_x
        y_out[k] = y + coef * lateral(y) - CORIOLIS * x - 0.1 * press_y
        below = centre > depth + 1.0
        up, down = lax.max(k - 1, 0), lax.min(k + 1, LEVELS - 1)
        for i, cells, out in ((2, t, t_out), (3, s, s_out)):
            vertical = (big[i, up] - cells) + jnp.where(below, big[i, down] - cells, 0.0)
            out[k] = cells + coef * lateral(cells) + DIAPYCNAL * vertical
        return press, sum_x + jnp.where(wet, x, 0.0), sum_y + jnp.where(wet, y, 0.0)

    _, sum_x, sum_y = lax.fori_loop(0, LEVELS, inner, (zero, zero, zero), unroll=LEVELS)
    count = jnp.maximum(centre, 1.0)
    mean_x, mean_y = sum_x / count, sum_y / count

    for sign, a, o, lead, _ in neighbours:

        @pl.when(lead == 1)
        def _(sign=sign, a=a, o=o):
            halo(sign, -a, -o).wait_recv()
            halo(sign, a, o).start()
            if adjacent(sign):
                deep_edge(sign, a, o).start()

    for sign, a, o, lead, _ in neighbours:

        @pl.when(lead == 0)
        def _(sign=sign, a=a, o=o):
            halo(sign, -a, -o).wait_recv()

    fields = [[], [], [], []]
    for a in (-2, -1, 0, 1, 2):
        inside = (lat + a >= 0) & (lat + a < lats)
        keep = jnp.where(inside, 1.0, 0.0).astype(f32)
        merged = jnp.where(lane % 32 < EDGE, side_recv[a + 2], side_recv[a + 7])
        for i in range(4):
            middle = own[i] if a == 0 else stack_recv[a + 2, i]
            beside = roll(merged, -(EDGE + 32 * i))
            if i == 0 and a != 0:
                middle, beside = middle * keep, beside * keep
            fields[i].append((middle, beside))
    halo_bottom = fields[0]

    def whole(tiles):
        return jnp.concatenate(
            [jnp.concatenate([m for m, _ in tiles], 0), jnp.concatenate([b for _, b in tiles], 0)], 1
        )

    def turn(cells, shift):
        return pltpu.roll(cells, shift % (2 * COLS), 1)

    def ns(cells):
        return pltpu.roll(cells, cells.shape[0] - 1, 0) - pltpu.roll(cells, 1, 0)

    column, level, flow_x, flow_y = (whole(tiles) for tiles in fields)
    wet = jnp.where(column > 0.0, 1.0, 0.0)
    gain = (WAVE / LEVELS) * column
    level, flow_x, flow_y = wet * level, wet * flow_x, wet * flow_y
    wet_e, wet_w = turn(wet, -1), turn(wet, 1)
    for cycle in range(SUBCYCLES):
        flux_x = gain * flow_x
        part = level - wet * ns(gain * flow_y)
        level = part - wet * (turn(flux_x, -1) - turn(flux_x, 1))
        slope_x = (turn(part, -1) - wet_e * (turn(flux_x, -2) - flux_x)) - (
            turn(part, 1) - wet_w * (flux_x - turn(flux_x, 2))
        )
        flow_x, flow_y = (
            flow_x - gain * slope_x + CORIOLIS * flow_y,
            flow_y - gain * ns(level) - CORIOLIS * flow_x,
        )
        if cycle == 3:
            wet, wet_e, wet_w, gain, level, flow_x, flow_y = (
                cells[ROWS : 4 * ROWS]
                for cells in (wet, wet_e, wet_w, gain, level, flow_x, flow_y)
            )
    level, flow_x, flow_y = (cells[ROWS : 2 * ROWS, :COLS] for cells in (level, flow_x, flow_y))
    flat_out[0] = level
    flat_out[1] = flow_x
    flat_out[2] = flow_y

    for sign, a, o, _, _ in neighbours:
        if adjacent(sign):
            deep_edge(sign, -a, -o).wait_recv()

    beside = halo_bottom[2][1]
    bottom_ew = jnp.where(
        lane == COLS - 1, roll(beside, -1), jnp.where(lane == 0, roll(beside, 1), 0.0)
    )
    bottom_ns = jnp.where(
        row == ROWS - 1,
        slide(halo_bottom[3][0], -1),
        jnp.where(row == 0, slide(halo_bottom[1][0], 1), 0.0),
    )
    from_west, from_east = cols_recv[0], cols_recv[1]
    first = jnp.where(even, from_east, roll(from_west, 1))
    second = jnp.where(even, roll(from_east, -1), from_west)
    sign_ew = jnp.where(lane == COLS - 1, 1.0, -1.0)
    sign_ns = jnp.where(row == ROWS - 1, 1.0, -1.0)
    t_ew, s_ew = 0.08 * sign_ew, -0.06 * sign_ew
    t_ns, s_ns = 0.08 * sign_ns, -0.06 * sign_ns
    add_x, add_y = flow_x - mean_x, flow_y - mean_y
    upper = row < ROWS // 2

    def outer(k, carry):
        press_ew, press_ns = carry
        depth = lax.convert_element_type(k, f32)
        wet = centre > depth
        wet_ew, wet_ns = bottom_ew > depth, bottom_ns > depth
        sides = [
            pltpu.roll(source, (COLS - 1 - 2 * (k + base)) % COLS, 1)
            for source, base in ((first, 0), (first, 32), (second, 0), (second, 32))
        ]
        stacks = [
            jnp.where(
                upper,
                jnp.broadcast_to(rows_recv[0, pl.ds(i * LEVELS + k, 1), :], (ROWS, COLS)),
                jnp.broadcast_to(rows_recv[1, pl.ds(i * LEVELS + k, 1), :], (ROWS, COLS)),
            )
            for i in range(4)
        ]

        def lateral(i):
            cells = big[i, k]
            return jnp.where(wet_ew, sides[i] - cells, 0.0) + jnp.where(
                wet_ns, stacks[i] - cells, 0.0
            )

        press_ew = press_ew + jnp.where(wet_ew, t_ew * sides[2] + s_ew * sides[3], 0.0)
        press_ns = press_ns + jnp.where(wet_ns, t_ns * stacks[2] + s_ns * stacks[3], 0.0)
        x_out[k] = jnp.where(wet, x_out[k] + coef * lateral(0) + (press_ew + add_x), 0.0)
        y_out[k] = jnp.where(wet, y_out[k] + coef * lateral(1) + (press_ns + add_y), 0.0)
        t_out[k] = jnp.where(wet, t_out[k] + coef * lateral(2), 0.0)
        s_out[k] = jnp.where(wet, s_out[k] + coef * lateral(3), 0.0)
        return press_ew, press_ns

    lax.fori_loop(0, LEVELS, outer, (zero, zero), unroll=LEVELS)

    for sign, a, o, _, _ in neighbours:
        halo(sign, a, o).wait_send()
        if adjacent(sign):
            deep_edge(sign, a, o).wait_send()


def store(flat, x, y, t, s, *rest):
    outs, sem = rest[:-1], rest[-1]
    sources = [flat.at[i] for i in range(3)] + [x, y, t, s]
    copies = [
        pltpu.make_async_copy(source, out, sem.at[i])
        for i, (source, out) in enumerate(zip(sources, outs))
    ]
    for copy in copies:
        copy.start()
    for copy in copies:
        copy.wait()


def body(*args):
    flat = jax.ShapeDtypeStruct((ROWS, COLS), f32)
    deep = jax.ShapeDtypeStruct((LEVELS, ROWS, COLS), f32)
    messages = 19
    args = [pltpu.with_memory_space_constraint(arg, pltpu.HBM) for arg in args]
    held = pl.pallas_call(
        kernel,
        out_shape=(pltpu.VMEM((3, ROWS, COLS), f32),)
        + (pltpu.VMEM((LEVELS, ROWS, COLS), f32),) * 4,
        in_specs=[pl.BlockSpec(memory_space=pltpu.HBM)] * 8,
        out_specs=(pl.BlockSpec(memory_space=pltpu.VMEM),) * 5,
        scratch_shapes=[
            pltpu.VMEM((ROWS, COLS), jnp.int32),
            pltpu.VMEM((4, ROWS, COLS), f32),
            pltpu.VMEM((4, LEVELS, ROWS, COLS), f32),
            pltpu.VMEM((ROWS, COLS), f32),
            pltpu.VMEM((10, ROWS, COLS), f32),
            pltpu.VMEM((5, 4, ROWS, COLS), f32),
            pltpu.VMEM((2, 4 * LEVELS, COLS), f32),
            pltpu.VMEM((2, 4 * LEVELS, COLS), f32),
            pltpu.VMEM((2, ROWS, COLS), f32),
            pltpu.VMEM((2, ROWS, COLS), f32),
            pltpu.SemaphoreType.DMA((8,)),
            pltpu.SemaphoreType.DMA((messages,)),
            pltpu.SemaphoreType.DMA((messages,)),
        ],
        compiler_params=pltpu.CompilerParams(
            collective_id=0, has_side_effects=True, vmem_limit_bytes=16 * 1024 * 1024
        ),
        name="step",
    )(*args)
    return pl.pallas_call(
        store,
        out_shape=(flat,) * 3 + (deep,) * 4,
        in_specs=[pl.BlockSpec(memory_space=pltpu.VMEM)] * 5,
        out_specs=(pl.BlockSpec(memory_space=pltpu.HBM),) * 7,
        scratch_shapes=[pltpu.SemaphoreType.DMA((7,))],
        compiler_params=pltpu.CompilerParams(vmem_limit_bytes=1024 * 1024),
        name="store",
    )(*(pltpu.with_memory_space_constraint(cells, pltpu.VMEM) for cells in held))


def solution(mesh):
    flat, deep = P("lat", "lon"), P(None, "lat", "lon")
    return jax.shard_map(
        body,
        mesh=mesh,
        in_specs=(flat,) * 4 + (deep,) * 4,
        out_specs=(flat,) * 3 + (deep,) * 4,
        check_vma=False,
    )
```

```python
import jax
import jax.numpy as jnp
from jax import lax
from jax.experimental import pallas as pl
from jax.experimental.pallas import tpu as pltpu
from jax.sharding import PartitionSpec as P

LEVELS = 32
SUBCYCLES = 8
ROWS = 8
COLS = 128
EDGE = 16
WAVE = 0.45
CORIOLIS = 0.12
DIAPYCNAL = 0.2

LATS = (-2, -1, 0, 1, 2)
OFFSETS = (
    (0, 1), (1, 0), (1, 1), (2, 0), (2, 1),
    (-1, 0), (-1, 1), (-2, 0), (-2, 1),
    (0, -1), (1, -1), (2, -1), (-1, -1), (-2, -1),
)
f32 = jnp.float32


def kernel(
    bottom_hbm, level_hbm, flow_x_hbm, flow_y_hbm, x_hbm, y_hbm, t_hbm, s_hbm,
    flat_out, x_out, y_out, t_out, s_out,
    bottom, own, big, edge, side_recv, stack_recv,
    rows_send, rows_recv, cols_send, cols_recv,
    local_sem, send_sem, recv_sem,
):
    lat, lon = lax.axis_index("lat"), lax.axis_index("lon")
    lats, lons = lax.axis_size("lat"), lax.axis_size("lon")

    small = [
        pltpu.make_async_copy(bottom_hbm, bottom, local_sem.at[0]),
        pltpu.make_async_copy(level_hbm, own.at[1], local_sem.at[1]),
        pltpu.make_async_copy(flow_x_hbm, own.at[2], local_sem.at[2]),
        pltpu.make_async_copy(flow_y_hbm, own.at[3], local_sem.at[3]),
    ]
    large = [
        pltpu.make_async_copy(ref, big.at[i], local_sem.at[4 + i])
        for i, ref in enumerate((x_hbm, y_hbm, t_hbm, s_hbm))
    ]
    for copy in small + large:
        copy.start()

    def flag(condition):
        return jnp.where(condition, 1, 0)

    spot, core = lax.rem(lat, 8), lax.rem(lon, 2)
    within = lax.rem(lon, 8)
    seam = flag(within == 0) + flag(within == 7)
    western = lax.rem(lax.div(lon, 8) + 3 + core, 4)
    up, across = 1 - 2 * flag(spot >= 4), 1 - 2 * core

    def roles(a_sign, o_sign):
        a, o = a_sign * up, o_sign * across
        if o_sign == 0:
            lead = flag(spot < lax.rem(lat + a + lats, 8))
            return a, o, lead, 1 - lead
        beyond = flag(spot + a < 0) + flag(spot + a >= 8)
        near = jnp.where(
            beyond == 0,
            core,
            jnp.where(lax.div(lon, 8) == 3, flag(o < 0), flag(spot < lax.rem(lat + a + lats, 8))),
        )
        if o_sign == 1:
            return a, o, near, 1 - near
        far = core * flag(spot + a < 0) + (1 - core) * flag(spot + a >= 8)
        west = flag(western == 0) + flag(western == 1) * (1 - far)
        east = flag(western == 3)
        lead = core * west + (1 - core) * east
        trail = core * east + (1 - core) * west
        return a, o, jnp.where(seam == 1, lead, near), jnp.where(seam == 1, trail, 1 - near)

    def is_first(a, o):
        return flag(lax.rem(lat + a + lats, lats) + lax.rem(lon + o + lons, lons) == 0)

    def awaits(a, o):
        there = lax.rem(lon + o + lons, lons)
        return flag(there == 24) * flag(lax.rem(lat + a + lats, 8) >= 6)

    def settled(a_sign, o_sign):
        a, o, lead, trail = roles(a_sign, o_sign)
        if o_sign != -1:
            lead = jnp.where(is_first(0, 0) == 1, 0, lead)
            trail = jnp.where(is_first(0, 0) == 1, 1, trail)
        if o_sign != -1:
            lead = jnp.where(awaits(0, 0) * flag(spot + a >= 8) == 1, 1, lead)
            trail = jnp.where(awaits(0, 0) * flag(spot + a >= 8) == 1, 0, trail)
        late = awaits(a, o) * flag(o != 1) * flag(spot + a < 0)
        lead, trail = jnp.where(late == 1, 0, lead), jnp.where(late == 1, 1, trail)
        first = is_first(a, o) * flag(o != 1)
        return a, o, jnp.where(first == 1, 1, lead), jnp.where(first == 1, 0, trail)

    neighbours = [(sign, *settled(*sign)) for sign in OFFSETS]

    def place(a, o):
        return {"lat": lax.rem(lat + a + lats, lats), "lon": lax.rem(lon + o + lons, lons)}

    barrier = pltpu.get_barrier_semaphore()
    for _, a, o, _, trail in neighbours[::-1]:

        @pl.when(trail == 0)
        def _(a=a, o=o):
            pl.semaphore_signal(
                barrier, inc=1, device_id=place(a, o), device_id_type=pl.DeviceIdType.MESH
            )

    awaited = sum(1 - lead for _, _, _, lead, _ in neighbours)

    lane = lax.broadcasted_iota(jnp.int32, (ROWS, COLS), 1)
    row = lax.broadcasted_iota(jnp.int32, (ROWS, COLS), 0)
    even = lane % 2 == 0

    def roll(cells, shift):
        return pltpu.roll(cells, shift % COLS, 1)

    def slide(cells, shift):
        return pltpu.roll(cells, shift % ROWS, 0)

    for copy in small:
        copy.wait()
    own[0] = bottom[...].astype(f32)
    packed = roll(own[0], EDGE)
    for i in range(1, 4):
        packed = jnp.where(lane // 32 == i, roll(own[i], EDGE + 32 * i), packed)
    edge[...] = packed

    def message(src, dst, index, a, o):
        return pltpu.make_async_remote_copy(
            src_ref=src,
            dst_ref=dst,
            send_sem=send_sem.at[index],
            recv_sem=recv_sem.at[index],
            device_id=place(a, o),
            device_id_type=pl.DeviceIdType.MESH,
        )

    def halo(sign, a, o):
        if sign[1] == 0:
            return message(own, stack_recv.at[2 - a], 12 - a, a, o)
        slot = 2 - a + 5 * lax.div(1 - o, 2)
        return message(edge, side_recv.at[slot], slot, a, o)

    def deep_edge(sign, a, o):
        if sign[1] == 0:
            there, slot = lax.div(a + 1, 2), lax.div(1 - a, 2)
            return message(rows_send.at[there], rows_recv.at[slot], 15 + slot, a, o)
        there, slot = lax.div(o + 1, 2), lax.div(1 - o, 2)
        return message(cols_send.at[there], cols_recv.at[slot], 17 + slot, a, o)

    def adjacent(sign):
        return abs(sign[0]) + abs(sign[1]) == 1

    @pl.when(awaited > 0)
    def _():
        pl.semaphore_wait(barrier, awaited)

    for sign, a, o, lead, _ in neighbours[::-1]:

        @pl.when(lead == 0)
        def _(sign=sign, a=a, o=o):
            halo(sign, a, o).start()

    for copy in large:
        copy.wait()
    for i in range(4):
        rows_send[0, pl.ds(i * LEVELS, LEVELS), :] = big[i, :, 0, :]
        rows_send[1, pl.ds(i * LEVELS, LEVELS), :] = big[i, :, ROWS - 1, :]

    def pack(k, carry):
        first, second = carry
        first = jnp.where(lane // 2 == k, pltpu.roll(big[0, k], 2 * k + 1, 1), first)
        first = jnp.where(lane // 2 == k + 32, pltpu.roll(big[1, k], 2 * k + 65, 1), first)
        second = jnp.where(lane // 2 == k, pltpu.roll(big[2, k], 2 * k + 1, 1), second)
        second = jnp.where(
            lane // 2 == k + 32, pltpu.roll(big[3, k], (2 * k + 65) % COLS, 1), second
        )
        return first, second

    zero = jnp.zeros((ROWS, COLS), f32)
    first, second = lax.fori_loop(0, LEVELS, pack, (zero, zero), unroll=LEVELS)
    cols_send[1] = jnp.where(even, first, roll(second, 1))
    cols_send[0] = jnp.where(even, roll(first, -1), second)

    for sign, a, o, lead, _ in neighbours:
        if adjacent(sign):

            @pl.when(lead == 0)
            def _(sign=sign, a=a, o=o):
                deep_edge(sign, a, o).start()

    centre = own[0]
    coef = 0.08 + (0.12 / LEVELS) * centre
    bottom_e = jnp.where(lane == COLS - 1, 0.0, roll(centre, -1))
    bottom_w = jnp.where(lane == 0, 0.0, roll(centre, 1))
    bottom_n = jnp.where(row == ROWS - 1, 0.0, slide(centre, -1))
    bottom_s = jnp.where(row == 0, 0.0, slide(centre, 1))

    def inner(k, carry):
        press, sum_x, sum_y = carry
        depth = lax.convert_element_type(k, f32)
        wet = centre > depth
        wet_e, wet_w = bottom_e > depth, bottom_w > depth
        wet_n, wet_s = bottom_n > depth, bottom_s > depth

        def lateral(cells):
            return (
                jnp.where(wet_e, roll(cells, -1), cells)
                + jnp.where(wet_w, roll(cells, 1), cells)
                + jnp.where(wet_n, slide(cells, -1), cells)
                + jnp.where(wet_s, slide(cells, 1), cells)
                - 4.0 * cells
            )

        x, y, t, s = big[0, k], big[1, k], big[2, k], big[3, k]
        press = press + jnp.where(wet, 0.6 * s - 0.8 * t, 0.0)
        press_x = jnp.where(lane == COLS - 1, 0.0, roll(press, -1)) - jnp.where(
            lane == 0, 0.0, roll(press, 1)
        )
        press_y = jnp.where(row == ROWS - 1, 0.0, slide(press, -1)) - jnp.where(
            row == 0, 0.0, slide(press, 1)
        )
        x_out[k] = x + coef * lateral(x) + CORIOLIS * y - 0.1 * press_x
        y_out[k] = y + coef * lateral(y) - CORIOLIS * x - 0.1 * press_y
        below = centre > depth + 1.0
        up, down = lax.max(k - 1, 0), lax.min(k + 1, LEVELS - 1)
        for i, cells, out in ((2, t, t_out), (3, s, s_out)):
            vertical = (big[i, up] - cells) + jnp.where(below, big[i, down] - cells, 0.0)
            out[k] = cells + coef * lateral(cells) + DIAPYCNAL * vertical
        return press, sum_x + jnp.where(wet, x, 0.0), sum_y + jnp.where(wet, y, 0.0)

    _, sum_x, sum_y = lax.fori_loop(0, LEVELS, inner, (zero, zero, zero), unroll=LEVELS)
    count = jnp.maximum(centre, 1.0)
    mean_x, mean_y = sum_x / count, sum_y / count

    for sign, a, o, lead, _ in neighbours:

        @pl.when(lead == 1)
        def _(sign=sign, a=a, o=o):
            halo(sign, -a, -o).wait_recv()
            halo(sign, a, o).start()
            if adjacent(sign):
                deep_edge(sign, a, o).start()

    for sign, a, o, lead, _ in neighbours:

        @pl.when(lead == 0)
        def _(sign=sign, a=a, o=o):
            halo(sign, -a, -o).wait_recv()

    for sign, a, o, _, _ in neighbours:
        if adjacent(sign):
            deep_edge(sign, -a, -o).wait_recv()

    fields = [[], [], [], []]
    for a in (-2, -1, 0, 1, 2):
        inside = (lat + a >= 0) & (lat + a < lats)
        keep = jnp.where(inside, 1.0, 0.0).astype(f32)
        merged = jnp.where(lane % 32 < EDGE, side_recv[a + 2], side_recv[a + 7])
        for i in range(4):
            middle = own[i] if a == 0 else stack_recv[a + 2, i]
            beside = roll(merged, -(EDGE + 32 * i))
            if i == 0 and a != 0:
                middle, beside = middle * keep, beside * keep
            fields[i].append((middle, beside))
    halo_bottom = fields[0]
    beside = halo_bottom[2][1]
    bottom_ew = jnp.where(
        lane == COLS - 1, roll(beside, -1), jnp.where(lane == 0, roll(beside, 1), 0.0)
    )
    bottom_ns = jnp.where(
        row == ROWS - 1,
        slide(halo_bottom[3][0], -1),
        jnp.where(row == 0, slide(halo_bottom[1][0], 1), 0.0),
    )
    from_west, from_east = cols_recv[0], cols_recv[1]
    first = jnp.where(even, from_east, roll(from_west, 1))
    second = jnp.where(even, roll(from_east, -1), from_west)
    sign_ew = jnp.where(lane == COLS - 1, 1.0, -1.0)
    sign_ns = jnp.where(row == ROWS - 1, 1.0, -1.0)
    t_ew, s_ew = 0.08 * sign_ew, -0.06 * sign_ew
    t_ns, s_ns = 0.08 * sign_ns, -0.06 * sign_ns
    upper = row < ROWS // 2

    def outer(k, carry):
        press_ew, press_ns = carry
        depth = lax.convert_element_type(k, f32)
        wet = centre > depth
        wet_ew, wet_ns = bottom_ew > depth, bottom_ns > depth
        sides = [
            pltpu.roll(source, (COLS - 1 - 2 * (k + base)) % COLS, 1)
            for source, base in ((first, 0), (first, 32), (second, 0), (second, 32))
        ]
        stacks = [
            jnp.where(
                upper,
                jnp.broadcast_to(rows_recv[0, pl.ds(i * LEVELS + k, 1), :], (ROWS, COLS)),
                jnp.broadcast_to(rows_recv[1, pl.ds(i * LEVELS + k, 1), :], (ROWS, COLS)),
            )
            for i in range(4)
        ]

        def lateral(i):
            cells = big[i, k]
            return jnp.where(wet_ew, sides[i] - cells, 0.0) + jnp.where(
                wet_ns, stacks[i] - cells, 0.0
            )

        press_ew = press_ew + jnp.where(wet_ew, t_ew * sides[2] + s_ew * sides[3], 0.0)
        press_ns = press_ns + jnp.where(wet_ns, t_ns * stacks[2] + s_ns * stacks[3], 0.0)
        x_out[k] = x_out[k] + coef * lateral(0) + press_ew
        y_out[k] = y_out[k] + coef * lateral(1) + press_ns
        t_out[k] = jnp.where(wet, t_out[k] + coef * lateral(2), 0.0)
        s_out[k] = jnp.where(wet, s_out[k] + coef * lateral(3), 0.0)
        return press_ew, press_ns

    edge_press = (zero, zero)


    def whole(tiles):
        return jnp.concatenate(
            [jnp.concatenate([m for m, _ in tiles], 0), jnp.concatenate([b for _, b in tiles], 0)], 1
        )

    def turn(cells, shift):
        return pltpu.roll(cells, shift % (2 * COLS), 1)

    def ns(cells):
        return pltpu.roll(cells, cells.shape[0] - 1, 0) - pltpu.roll(cells, 1, 0)

    column, level, flow_x, flow_y = (whole(tiles) for tiles in fields)
    wet = jnp.where(column > 0.0, 1.0, 0.0)
    gain = (WAVE / LEVELS) * column
    level, flow_x, flow_y = wet * level, wet * flow_x, wet * flow_y
    wet_e, wet_w = turn(wet, -1), turn(wet, 1)
    for cycle in range(SUBCYCLES):
        flux_x = gain * flow_x
        part = level - wet * ns(gain * flow_y)
        level = part - wet * (turn(flux_x, -1) - turn(flux_x, 1))
        slope_x = (turn(part, -1) - wet_e * (turn(flux_x, -2) - flux_x)) - (
            turn(part, 1) - wet_w * (flux_x - turn(flux_x, 2))
        )
        flow_x, flow_y = (
            flow_x - gain * slope_x + CORIOLIS * flow_y,
            flow_y - gain * ns(level) - CORIOLIS * flow_x,
        )
        edge_press = lax.fori_loop(4 * cycle, 4 * cycle + 4, outer, edge_press, unroll=4)
        if cycle == 3:
            wet, wet_e, wet_w, gain, level, flow_x, flow_y = (
                cells[ROWS : 4 * ROWS]
                for cells in (wet, wet_e, wet_w, gain, level, flow_x, flow_y)
            )
    level, flow_x, flow_y = (cells[ROWS : 2 * ROWS, :COLS] for cells in (level, flow_x, flow_y))
    flat_out[0] = level
    flat_out[1] = flow_x
    flat_out[2] = flow_y

    add_x, add_y = flow_x - mean_x, flow_y - mean_y

    def finish(k, carry):
        wet = centre > lax.convert_element_type(k, f32)
        x_out[k] = jnp.where(wet, x_out[k] + add_x, 0.0)
        y_out[k] = jnp.where(wet, y_out[k] + add_y, 0.0)
        return carry

    lax.fori_loop(0, LEVELS, finish, 0, unroll=LEVELS)

    for sign, a, o, _, _ in neighbours:
        halo(sign, a, o).wait_send()
        if adjacent(sign):
            deep_edge(sign, a, o).wait_send()


def store(flat, x, y, t, s, *rest):
    outs, sem = rest[:-1], rest[-1]
    sources = [flat.at[i] for i in range(3)] + [x, y, t, s]
    copies = [
        pltpu.make_async_copy(source, out, sem.at[i])
        for i, (source, out) in enumerate(zip(sources, outs))
    ]
    for copy in copies:
        copy.start()
    for copy in copies:
        copy.wait()


def body(*args):
    flat = jax.ShapeDtypeStruct((ROWS, COLS), f32)
    deep = jax.ShapeDtypeStruct((LEVELS, ROWS, COLS), f32)
    messages = 19
    args = [pltpu.with_memory_space_constraint(arg, pltpu.HBM) for arg in args]
    held = pl.pallas_call(
        kernel,
        out_shape=(pltpu.VMEM((3, ROWS, COLS), f32),)
        + (pltpu.VMEM((LEVELS, ROWS, COLS), f32),) * 4,
        in_specs=[pl.BlockSpec(memory_space=pltpu.HBM)] * 8,
        out_specs=(pl.BlockSpec(memory_space=pltpu.VMEM),) * 5,
        scratch_shapes=[
            pltpu.VMEM((ROWS, COLS), jnp.int32),
            pltpu.VMEM((4, ROWS, COLS), f32),
            pltpu.VMEM((4, LEVELS, ROWS, COLS), f32),
            pltpu.VMEM((ROWS, COLS), f32),
            pltpu.VMEM((10, ROWS, COLS), f32),
            pltpu.VMEM((5, 4, ROWS, COLS), f32),
            pltpu.VMEM((2, 4 * LEVELS, COLS), f32),
            pltpu.VMEM((2, 4 * LEVELS, COLS), f32),
            pltpu.VMEM((2, ROWS, COLS), f32),
            pltpu.VMEM((2, ROWS, COLS), f32),
            pltpu.SemaphoreType.DMA((8,)),
            pltpu.SemaphoreType.DMA((messages,)),
            pltpu.SemaphoreType.DMA((messages,)),
        ],
        compiler_params=pltpu.CompilerParams(
            collective_id=0, has_side_effects=True, vmem_limit_bytes=16 * 1024 * 1024
        ),
        name="step",
    )(*args)
    return pl.pallas_call(
        store,
        out_shape=(flat,) * 3 + (deep,) * 4,
        in_specs=[pl.BlockSpec(memory_space=pltpu.VMEM)] * 5,
        out_specs=(pl.BlockSpec(memory_space=pltpu.HBM),) * 7,
        scratch_shapes=[pltpu.SemaphoreType.DMA((7,))],
        compiler_params=pltpu.CompilerParams(vmem_limit_bytes=1024 * 1024),
        name="store",
    )(*(pltpu.with_memory_space_constraint(cells, pltpu.VMEM) for cells in held))


def solution(mesh):
    flat, deep = P("lat", "lon"), P(None, "lat", "lon")
    return jax.shard_map(
        body,
        mesh=mesh,
        in_specs=(flat,) * 4 + (deep,) * 4,
        out_specs=(flat,) * 3 + (deep,) * 4,
        check_vma=False,
    )
```

```python
import jax
import jax.numpy as jnp
from jax import lax
from jax.experimental import pallas as pl
from jax.experimental.pallas import tpu as pltpu
from jax.sharding import PartitionSpec as P

LEVELS = 32
SUBCYCLES = 8
ROWS = 8
COLS = 128
EDGE = 16
WAVE = 0.45
CORIOLIS = 0.12
DIAPYCNAL = 0.2

LATS = (-2, -1, 0, 1, 2)
OFFSETS = (
    (0, 1), (1, 0), (1, 1), (2, 0), (2, 1),
    (-1, 0), (-1, 1), (-2, 0), (-2, 1),
    (0, -1), (1, -1), (2, -1), (-1, -1), (-2, -1),
)
f32 = jnp.float32


def kernel(
    bottom_hbm, level_hbm, flow_x_hbm, flow_y_hbm, x_hbm, y_hbm, t_hbm, s_hbm,
    flat_out, x_out, y_out, t_out, s_out,
    bottom, own, big, edge, side_recv, stack_recv,
    rows_send, rows_recv, cols_send, cols_recv,
    local_sem, send_sem, recv_sem,
):
    lat, lon = lax.axis_index("lat"), lax.axis_index("lon")
    lats, lons = lax.axis_size("lat"), lax.axis_size("lon")

    small = [
        pltpu.make_async_copy(bottom_hbm, bottom, local_sem.at[0]),
        pltpu.make_async_copy(level_hbm, own.at[1], local_sem.at[1]),
        pltpu.make_async_copy(flow_x_hbm, own.at[2], local_sem.at[2]),
        pltpu.make_async_copy(flow_y_hbm, own.at[3], local_sem.at[3]),
    ]
    large = [
        pltpu.make_async_copy(ref, big.at[i], local_sem.at[4 + i])
        for i, ref in enumerate((x_hbm, y_hbm, t_hbm, s_hbm))
    ]
    for copy in small + large:
        copy.start()

    def flag(condition):
        return jnp.where(condition, 1, 0)

    spot, core = lax.rem(lat, 8), lax.rem(lon, 2)
    within = lax.rem(lon, 8)
    seam = flag(within == 0) + flag(within == 7)
    western = lax.rem(lax.div(lon, 8) + 3 + core, 4)
    up, across = 1 - 2 * flag(spot >= 4), 1 - 2 * core

    def roles(a_sign, o_sign):
        a, o = a_sign * up, o_sign * across
        if o_sign == 0:
            lead = flag(spot < lax.rem(lat + a + lats, 8))
            return a, o, lead, 1 - lead
        beyond = flag(spot + a < 0) + flag(spot + a >= 8)
        near = jnp.where(
            beyond == 0,
            core,
            jnp.where(lax.div(lon, 8) == 3, flag(o < 0), flag(spot < lax.rem(lat + a + lats, 8))),
        )
        if o_sign == 1:
            return a, o, near, 1 - near
        far = core * flag(spot + a < 0) + (1 - core) * flag(spot + a >= 8)
        west = flag(western == 0) + flag(western == 1) * (1 - far)
        east = flag(western == 3)
        lead = core * west + (1 - core) * east
        trail = core * east + (1 - core) * west
        return a, o, jnp.where(seam == 1, lead, near), jnp.where(seam == 1, trail, 1 - near)

    def is_first(a, o):
        return flag(lax.rem(lat + a + lats, lats) + lax.rem(lon + o + lons, lons) == 0)

    def awaits(a, o):
        there = lax.rem(lon + o + lons, lons)
        return flag(there == 24) * flag(lax.rem(lat + a + lats, 8) >= 6)

    def settled(a_sign, o_sign):
        a, o, lead, trail = roles(a_sign, o_sign)
        if o_sign != -1:
            lead = jnp.where(is_first(0, 0) == 1, 0, lead)
            trail = jnp.where(is_first(0, 0) == 1, 1, trail)
        if o_sign != -1:
            lead = jnp.where(awaits(0, 0) * flag(spot + a >= 8) == 1, 1, lead)
            trail = jnp.where(awaits(0, 0) * flag(spot + a >= 8) == 1, 0, trail)
        late = awaits(a, o) * flag(o != 1) * flag(spot + a < 0)
        lead, trail = jnp.where(late == 1, 0, lead), jnp.where(late == 1, 1, trail)
        if o_sign == 0:
            here = flag(lon == 8) * flag(spot + a >= 0) * flag(spot + a < 8)
            ahead = here * flag(spot >= 6) * flag(spot + a < 6)
            behind = here * flag(spot < 6) * flag(spot + a >= 6)
            lead = jnp.where(ahead == 1, 1, jnp.where(behind == 1, 0, lead))
            trail = jnp.where(ahead == 1, 0, jnp.where(behind == 1, 1, trail))
        first = is_first(a, o) * flag(o != 1)
        return a, o, jnp.where(first == 1, 1, lead), jnp.where(first == 1, 0, trail)

    neighbours = [(sign, *settled(*sign)) for sign in OFFSETS]

    def place(a, o):
        return {"lat": lax.rem(lat + a + lats, lats), "lon": lax.rem(lon + o + lons, lons)}

    barrier = pltpu.get_barrier_semaphore()
    for _, a, o, _, trail in neighbours[::-1]:

        @pl.when(trail == 0)
        def _(a=a, o=o):
            pl.semaphore_signal(
                barrier, inc=1, device_id=place(a, o), device_id_type=pl.DeviceIdType.MESH
            )

    awaited = sum(1 - lead for _, _, _, lead, _ in neighbours)

    lane = lax.broadcasted_iota(jnp.int32, (ROWS, COLS), 1)
    row = lax.broadcasted_iota(jnp.int32, (ROWS, COLS), 0)
    even = lane % 2 == 0

    def roll(cells, shift):
        return pltpu.roll(cells, shift % COLS, 1)

    def slide(cells, shift):
        return pltpu.roll(cells, shift % ROWS, 0)

    for copy in small:
        copy.wait()
    own[0] = bottom[...].astype(f32)
    packed = roll(own[0], EDGE)
    for i in range(1, 4):
        packed = jnp.where(lane // 32 == i, roll(own[i], EDGE + 32 * i), packed)
    edge[...] = packed

    def message(src, dst, index, a, o):
        return pltpu.make_async_remote_copy(
            src_ref=src,
            dst_ref=dst,
            send_sem=send_sem.at[index],
            recv_sem=recv_sem.at[index],
            device_id=place(a, o),
            device_id_type=pl.DeviceIdType.MESH,
        )

    def halo(sign, a, o):
        if sign[1] == 0:
            return message(own, stack_recv.at[2 - a], 12 - a, a, o)
        slot = 2 - a + 5 * lax.div(1 - o, 2)
        return message(edge, side_recv.at[slot], slot, a, o)

    def deep_edge(sign, a, o):
        if sign[1] == 0:
            there, slot = lax.div(a + 1, 2), lax.div(1 - a, 2)
            return message(rows_send.at[there], rows_recv.at[slot], 15 + slot, a, o)
        there, slot = lax.div(o + 1, 2), lax.div(1 - o, 2)
        return message(cols_send.at[there], cols_recv.at[slot], 17 + slot, a, o)

    def adjacent(sign):
        return abs(sign[0]) + abs(sign[1]) == 1

    @pl.when(awaited > 0)
    def _():
        pl.semaphore_wait(barrier, awaited)

    for sign, a, o, lead, _ in neighbours[::-1]:

        @pl.when(lead == 0)
        def _(sign=sign, a=a, o=o):
            halo(sign, a, o).start()

    for copy in large:
        copy.wait()
    for i in range(4):
        rows_send[0, pl.ds(i * LEVELS, LEVELS), :] = big[i, :, 0, :]
        rows_send[1, pl.ds(i * LEVELS, LEVELS), :] = big[i, :, ROWS - 1, :]

    def pack(k, carry):
        first, second = carry
        first = jnp.where(lane // 2 == k, pltpu.roll(big[0, k], 2 * k + 1, 1), first)
        first = jnp.where(lane // 2 == k + 32, pltpu.roll(big[1, k], 2 * k + 65, 1), first)
        second = jnp.where(lane // 2 == k, pltpu.roll(big[2, k], 2 * k + 1, 1), second)
        second = jnp.where(
            lane // 2 == k + 32, pltpu.roll(big[3, k], (2 * k + 65) % COLS, 1), second
        )
        return first, second

    zero = jnp.zeros((ROWS, COLS), f32)
    first, second = lax.fori_loop(0, LEVELS, pack, (zero, zero), unroll=LEVELS)
    cols_send[1] = jnp.where(even, first, roll(second, 1))
    cols_send[0] = jnp.where(even, roll(first, -1), second)

    for sign, a, o, lead, _ in neighbours:
        if adjacent(sign):

            @pl.when(lead == 0)
            def _(sign=sign, a=a, o=o):
                deep_edge(sign, a, o).start()

    centre = own[0]
    coef = 0.08 + (0.12 / LEVELS) * centre
    bottom_e = jnp.where(lane == COLS - 1, 0.0, roll(centre, -1))
    bottom_w = jnp.where(lane == 0, 0.0, roll(centre, 1))
    bottom_n = jnp.where(row == ROWS - 1, 0.0, slide(centre, -1))
    bottom_s = jnp.where(row == 0, 0.0, slide(centre, 1))

    def inner(k, carry):
        press, sum_x, sum_y = carry
        depth = lax.convert_element_type(k, f32)
        wet = centre > depth
        wet_e, wet_w = bottom_e > depth, bottom_w > depth
        wet_n, wet_s = bottom_n > depth, bottom_s > depth

        def lateral(cells):
            return (
                jnp.where(wet_e, roll(cells, -1), cells)
                + jnp.where(wet_w, roll(cells, 1), cells)
                + jnp.where(wet_n, slide(cells, -1), cells)
                + jnp.where(wet_s, slide(cells, 1), cells)
                - 4.0 * cells
            )

        x, y, t, s = big[0, k], big[1, k], big[2, k], big[3, k]
        press = press + jnp.where(wet, 0.6 * s - 0.8 * t, 0.0)
        press_x = jnp.where(lane == COLS - 1, 0.0, roll(press, -1)) - jnp.where(
            lane == 0, 0.0, roll(press, 1)
        )
        press_y = jnp.where(row == ROWS - 1, 0.0, slide(press, -1)) - jnp.where(
            row == 0, 0.0, slide(press, 1)
        )
        x_out[k] = x + coef * lateral(x) + CORIOLIS * y - 0.1 * press_x
        y_out[k] = y + coef * lateral(y) - CORIOLIS * x - 0.1 * press_y
        below = centre > depth + 1.0
        up, down = lax.max(k - 1, 0), lax.min(k + 1, LEVELS - 1)
        for i, cells, out in ((2, t, t_out), (3, s, s_out)):
            vertical = (big[i, up] - cells) + jnp.where(below, big[i, down] - cells, 0.0)
            out[k] = cells + coef * lateral(cells) + DIAPYCNAL * vertical
        return press, sum_x + jnp.where(wet, x, 0.0), sum_y + jnp.where(wet, y, 0.0)

    _, sum_x, sum_y = lax.fori_loop(0, LEVELS, inner, (zero, zero, zero), unroll=LEVELS)
    count = jnp.maximum(centre, 1.0)
    mean_x, mean_y = sum_x / count, sum_y / count

    for sign, a, o, lead, _ in neighbours:

        @pl.when(lead == 1)
        def _(sign=sign, a=a, o=o):
            halo(sign, -a, -o).wait_recv()
            halo(sign, a, o).start()
            if adjacent(sign):
                deep_edge(sign, a, o).start()

    for sign, a, o, lead, _ in neighbours:

        @pl.when(lead == 0)
        def _(sign=sign, a=a, o=o):
            halo(sign, -a, -o).wait_recv()

    for sign, a, o, _, _ in neighbours:
        if adjacent(sign):
            deep_edge(sign, -a, -o).wait_recv()

    fields = [[], [], [], []]
    for a in (-2, -1, 0, 1, 2):
        inside = (lat + a >= 0) & (lat + a < lats)
        keep = jnp.where(inside, 1.0, 0.0).astype(f32)
        merged = jnp.where(lane % 32 < EDGE, side_recv[a + 2], side_recv[a + 7])
        for i in range(4):
            middle = own[i] if a == 0 else stack_recv[a + 2, i]
            beside = roll(merged, -(EDGE + 32 * i))
            if i == 0 and a != 0:
                middle, beside = middle * keep, beside * keep
            fields[i].append((middle, beside))
    halo_bottom = fields[0]
    beside = halo_bottom[2][1]
    bottom_ew = jnp.where(
        lane == COLS - 1, roll(beside, -1), jnp.where(lane == 0, roll(beside, 1), 0.0)
    )
    bottom_ns = jnp.where(
        row == ROWS - 1,
        slide(halo_bottom[3][0], -1),
        jnp.where(row == 0, slide(halo_bottom[1][0], 1), 0.0),
    )
    from_west, from_east = cols_recv[0], cols_recv[1]
    first = jnp.where(even, from_east, roll(from_west, 1))
    second = jnp.where(even, roll(from_east, -1), from_west)
    sign_ew = jnp.where(lane == COLS - 1, 1.0, -1.0)
    sign_ns = jnp.where(row == ROWS - 1, 1.0, -1.0)
    t_ew, s_ew = 0.08 * sign_ew, -0.06 * sign_ew
    t_ns, s_ns = 0.08 * sign_ns, -0.06 * sign_ns
    upper = row < ROWS // 2

    def outer(k, carry):
        press_ew, press_ns = carry
        depth = lax.convert_element_type(k, f32)
        wet = centre > depth
        wet_ew, wet_ns = bottom_ew > depth, bottom_ns > depth
        sides = [
            pltpu.roll(source, (COLS - 1 - 2 * (k + base)) % COLS, 1)
            for source, base in ((first, 0), (first, 32), (second, 0), (second, 32))
        ]
        stacks = [
            jnp.where(
                upper,
                jnp.broadcast_to(rows_recv[0, pl.ds(i * LEVELS + k, 1), :], (ROWS, COLS)),
                jnp.broadcast_to(rows_recv[1, pl.ds(i * LEVELS + k, 1), :], (ROWS, COLS)),
            )
            for i in range(4)
        ]

        def lateral(i):
            cells = big[i, k]
            return jnp.where(wet_ew, sides[i] - cells, 0.0) + jnp.where(
                wet_ns, stacks[i] - cells, 0.0
            )

        press_ew = press_ew + jnp.where(wet_ew, t_ew * sides[2] + s_ew * sides[3], 0.0)
        press_ns = press_ns + jnp.where(wet_ns, t_ns * stacks[2] + s_ns * stacks[3], 0.0)
        x_out[k] = x_out[k] + coef * lateral(0) + press_ew
        y_out[k] = y_out[k] + coef * lateral(1) + press_ns
        t_out[k] = jnp.where(wet, t_out[k] + coef * lateral(2), 0.0)
        s_out[k] = jnp.where(wet, s_out[k] + coef * lateral(3), 0.0)
        return press_ew, press_ns

    edge_press = (zero, zero)


    def whole(tiles):
        return jnp.concatenate(
            [jnp.concatenate([m for m, _ in tiles], 0), jnp.concatenate([b for _, b in tiles], 0)], 1
        )

    def turn(cells, shift):
        return pltpu.roll(cells, shift % (2 * COLS), 1)

    def ns(cells):
        return pltpu.roll(cells, cells.shape[0] - 1, 0) - pltpu.roll(cells, 1, 0)

    column, level, flow_x, flow_y = (whole(tiles) for tiles in fields)
    wet = jnp.where(column > 0.0, 1.0, 0.0)
    gain = (WAVE / LEVELS) * column
    level, flow_x, flow_y = wet * level, wet * flow_x, wet * flow_y
    wet_e, wet_w = turn(wet, -1), turn(wet, 1)
    for cycle in range(SUBCYCLES):
        flux_x = gain * flow_x
        part = level - wet * ns(gain * flow_y)
        level = part - wet * (turn(flux_x, -1) - turn(flux_x, 1))
        slope_x = (turn(part, -1) - wet_e * (turn(flux_x, -2) - flux_x)) - (
            turn(part, 1) - wet_w * (flux_x - turn(flux_x, 2))
        )
        flow_x, flow_y = (
            flow_x - gain * slope_x + CORIOLIS * flow_y,
            flow_y - gain * ns(level) - CORIOLIS * flow_x,
        )
        edge_press = lax.fori_loop(4 * cycle, 4 * cycle + 4, outer, edge_press, unroll=4)
        if cycle == 3:
            wet, wet_e, wet_w, gain, level, flow_x, flow_y = (
                cells[ROWS : 4 * ROWS]
                for cells in (wet, wet_e, wet_w, gain, level, flow_x, flow_y)
            )
    level, flow_x, flow_y = (cells[ROWS : 2 * ROWS, :COLS] for cells in (level, flow_x, flow_y))
    flat_out[0] = level
    flat_out[1] = flow_x
    flat_out[2] = flow_y

    add_x, add_y = flow_x - mean_x, flow_y - mean_y

    def finish(k, carry):
        wet = centre > lax.convert_element_type(k, f32)
        x_out[k] = jnp.where(wet, x_out[k] + add_x, 0.0)
        y_out[k] = jnp.where(wet, y_out[k] + add_y, 0.0)
        return carry

    lax.fori_loop(0, LEVELS, finish, 0, unroll=LEVELS)

    for sign, a, o, _, _ in neighbours:
        halo(sign, a, o).wait_send()
        if adjacent(sign):
            deep_edge(sign, a, o).wait_send()


def store(flat, x, y, t, s, *rest):
    outs, sem = rest[:-1], rest[-1]
    sources = [flat.at[i] for i in range(3)] + [x, y, t, s]
    copies = [
        pltpu.make_async_copy(source, out, sem.at[i])
        for i, (source, out) in enumerate(zip(sources, outs))
    ][::-1]
    for copy in copies:
        copy.start()
    for copy in copies:
        copy.wait()


def body(*args):
    flat = jax.ShapeDtypeStruct((ROWS, COLS), f32)
    deep = jax.ShapeDtypeStruct((LEVELS, ROWS, COLS), f32)
    messages = 19
    args = [pltpu.with_memory_space_constraint(arg, pltpu.HBM) for arg in args]
    held = pl.pallas_call(
        kernel,
        out_shape=(pltpu.VMEM((3, ROWS, COLS), f32),)
        + (pltpu.VMEM((LEVELS, ROWS, COLS), f32),) * 4,
        in_specs=[pl.BlockSpec(memory_space=pltpu.HBM)] * 8,
        out_specs=(pl.BlockSpec(memory_space=pltpu.VMEM),) * 5,
        scratch_shapes=[
            pltpu.VMEM((ROWS, COLS), jnp.int32),
            pltpu.VMEM((4, ROWS, COLS), f32),
            pltpu.VMEM((4, LEVELS, ROWS, COLS), f32),
            pltpu.VMEM((ROWS, COLS), f32),
            pltpu.VMEM((10, ROWS, COLS), f32),
            pltpu.VMEM((5, 4, ROWS, COLS), f32),
            pltpu.VMEM((2, 4 * LEVELS, COLS), f32),
            pltpu.VMEM((2, 4 * LEVELS, COLS), f32),
            pltpu.VMEM((2, ROWS, COLS), f32),
            pltpu.VMEM((2, ROWS, COLS), f32),
            pltpu.SemaphoreType.DMA((8,)),
            pltpu.SemaphoreType.DMA((messages,)),
            pltpu.SemaphoreType.DMA((messages,)),
        ],
        compiler_params=pltpu.CompilerParams(
            collective_id=0, has_side_effects=True, vmem_limit_bytes=16 * 1024 * 1024
        ),
        name="step",
    )(*args)
    return pl.pallas_call(
        store,
        out_shape=(flat,) * 3 + (deep,) * 4,
        in_specs=[pl.BlockSpec(memory_space=pltpu.VMEM)] * 5,
        out_specs=(pl.BlockSpec(memory_space=pltpu.HBM),) * 7,
        scratch_shapes=[pltpu.SemaphoreType.DMA((7,))],
        compiler_params=pltpu.CompilerParams(vmem_limit_bytes=1024 * 1024),
        name="store",
    )(*(pltpu.with_memory_space_constraint(cells, pltpu.VMEM) for cells in held))


def solution(mesh):
    flat, deep = P("lat", "lon"), P(None, "lat", "lon")
    return jax.shard_map(
        body,
        mesh=mesh,
        in_specs=(flat,) * 4 + (deep,) * 4,
        out_specs=(flat,) * 3 + (deep,) * 4,
        check_vma=False,
    )
```

```python
import jax
import jax.numpy as jnp
from jax import lax
from jax.experimental import pallas as pl
from jax.experimental.pallas import tpu as pltpu
from jax.sharding import PartitionSpec as P

LEVELS = 32
SUBCYCLES = 8
ROWS = 8
COLS = 128
EDGE = 16
WAVE = 0.45
CORIOLIS = 0.12
DIAPYCNAL = 0.2

LATS = (-2, -1, 0, 1, 2)
OFFSETS = (
    (0, 1), (1, 0), (1, 1), (2, 0), (2, 1),
    (-1, 0), (-1, 1), (-2, 0), (-2, 1),
    (0, -1), (1, -1), (2, -1), (-1, -1), (-2, -1),
)
f32 = jnp.float32


def kernel(
    bottom_hbm, level_hbm, flow_x_hbm, flow_y_hbm, x_hbm, y_hbm, t_hbm, s_hbm,
    flat_out, x_out, y_out, t_out, s_out,
    bottom, own, big, edge, side_recv, stack_recv,
    rows_send, rows_recv, cols_send, cols_recv,
    local_sem, send_sem, recv_sem,
):
    lat, lon = lax.axis_index("lat"), lax.axis_index("lon")
    lats, lons = lax.axis_size("lat"), lax.axis_size("lon")

    small = [
        pltpu.make_async_copy(bottom_hbm, bottom, local_sem.at[0]),
        pltpu.make_async_copy(level_hbm, own.at[1], local_sem.at[1]),
        pltpu.make_async_copy(flow_x_hbm, own.at[2], local_sem.at[2]),
        pltpu.make_async_copy(flow_y_hbm, own.at[3], local_sem.at[3]),
    ]
    large = [
        pltpu.make_async_copy(ref, big.at[i], local_sem.at[4 + i])
        for i, ref in enumerate((x_hbm, y_hbm, t_hbm, s_hbm))
    ]
    for copy in small + large:
        copy.start()

    def flag(condition):
        return jnp.where(condition, 1, 0)

    spot, core = lax.rem(lat, 8), lax.rem(lon, 2)
    within = lax.rem(lon, 8)
    seam = flag(within == 0) + flag(within == 7)
    western = lax.rem(lax.div(lon, 8) + 3 + core, 4)
    up, across = 1 - 2 * flag(spot >= 4), 1 - 2 * core

    def roles(a_sign, o_sign):
        a, o = a_sign * up, o_sign * across
        if o_sign == 0:
            lead = flag(spot < lax.rem(lat + a + lats, 8))
            return a, o, lead, 1 - lead
        beyond = flag(spot + a < 0) + flag(spot + a >= 8)
        near = jnp.where(
            beyond == 0,
            core,
            jnp.where(lax.div(lon, 8) == 3, flag(o < 0), flag(spot < lax.rem(lat + a + lats, 8))),
        )
        if o_sign == 1:
            return a, o, near, 1 - near
        far = core * flag(spot + a < 0) + (1 - core) * flag(spot + a >= 8)
        west = flag(western == 0) + flag(western == 1) * (1 - far)
        east = flag(western == 3)
        lead = core * west + (1 - core) * east
        trail = core * east + (1 - core) * west
        return a, o, jnp.where(seam == 1, lead, near), jnp.where(seam == 1, trail, 1 - near)

    def is_first(a, o):
        return flag(lax.rem(lat + a + lats, lats) + lax.rem(lon + o + lons, lons) == 0)

    def awaits(a, o):
        there = lax.rem(lon + o + lons, lons)
        return flag(there == 24) * flag(lax.rem(lat + a + lats, 8) >= 6)

    def settled(a_sign, o_sign):
        a, o, lead, trail = roles(a_sign, o_sign)
        if o_sign != -1:
            lead = jnp.where(is_first(0, 0) == 1, 0, lead)
            trail = jnp.where(is_first(0, 0) == 1, 1, trail)
        if o_sign != -1:
            lead = jnp.where(awaits(0, 0) * flag(spot + a >= 8) == 1, 1, lead)
            trail = jnp.where(awaits(0, 0) * flag(spot + a >= 8) == 1, 0, trail)
        late = awaits(a, o) * flag(o != 1) * flag(spot + a < 0)
        lead, trail = jnp.where(late == 1, 0, lead), jnp.where(late == 1, 1, trail)
        if o_sign == 0:
            here = flag(lon == 8) * flag(spot + a >= 0) * flag(spot + a < 8)
            ahead = here * flag(spot >= 6) * flag(spot + a < 6)
            behind = here * flag(spot < 6) * flag(spot + a >= 6)
            lead = jnp.where(ahead == 1, 1, jnp.where(behind == 1, 0, lead))
            trail = jnp.where(ahead == 1, 0, jnp.where(behind == 1, 1, trail))
        first = is_first(a, o) * flag(o != 1)
        return a, o, jnp.where(first == 1, 1, lead), jnp.where(first == 1, 0, trail)

    neighbours = [(sign, *settled(*sign)) for sign in OFFSETS]

    def place(a, o):
        return {"lat": lax.rem(lat + a + lats, lats), "lon": lax.rem(lon + o + lons, lons)}

    barrier = pltpu.get_barrier_semaphore()
    for _, a, o, _, trail in neighbours[::-1]:

        @pl.when(trail == 0)
        def _(a=a, o=o):
            pl.semaphore_signal(
                barrier, inc=1, device_id=place(a, o), device_id_type=pl.DeviceIdType.MESH
            )

    awaited = sum(1 - lead for _, _, _, lead, _ in neighbours)

    lane = lax.broadcasted_iota(jnp.int32, (ROWS, COLS), 1)
    row = lax.broadcasted_iota(jnp.int32, (ROWS, COLS), 0)
    even = lane % 2 == 0

    def roll(cells, shift):
        return pltpu.roll(cells, shift % COLS, 1)

    def slide(cells, shift):
        return pltpu.roll(cells, shift % ROWS, 0)

    for copy in small:
        copy.wait()
    own[0] = bottom[...].astype(f32)
    packed = roll(own[0], EDGE)
    for i in range(1, 4):
        packed = jnp.where(lane // 32 == i, roll(own[i], EDGE + 32 * i), packed)
    edge[...] = packed

    def message(src, dst, index, a, o):
        return pltpu.make_async_remote_copy(
            src_ref=src,
            dst_ref=dst,
            send_sem=send_sem.at[index],
            recv_sem=recv_sem.at[index],
            device_id=place(a, o),
            device_id_type=pl.DeviceIdType.MESH,
        )

    def halo(sign, a, o):
        if sign[1] == 0:
            return message(own, stack_recv.at[2 - a], 12 - a, a, o)
        slot = 2 - a + 5 * lax.div(1 - o, 2)
        return message(edge, side_recv.at[slot], slot, a, o)

    def deep_edge(sign, a, o):
        if sign[1] == 0:
            there, slot = lax.div(a + 1, 2), lax.div(1 - a, 2)
            return message(rows_send.at[there], rows_recv.at[slot], 15 + slot, a, o)
        there, slot = lax.div(o + 1, 2), lax.div(1 - o, 2)
        return message(cols_send.at[there], cols_recv.at[slot], 17 + slot, a, o)

    def adjacent(sign):
        return abs(sign[0]) + abs(sign[1]) == 1

    @pl.when(awaited > 0)
    def _():
        pl.semaphore_wait(barrier, awaited)

    for sign, a, o, lead, _ in neighbours[-2:] + neighbours[-3::-1]:

        @pl.when(lead == 0)
        def _(sign=sign, a=a, o=o):
            halo(sign, a, o).start()

    for copy in large:
        copy.wait()
    for i in range(4):
        rows_send[0, pl.ds(i * LEVELS, LEVELS), :] = big[i, :, 0, :]
        rows_send[1, pl.ds(i * LEVELS, LEVELS), :] = big[i, :, ROWS - 1, :]

    def pack(k, carry):
        first, second = carry
        first = jnp.where(lane // 2 == k, pltpu.roll(big[0, k], 2 * k + 1, 1), first)
        first = jnp.where(lane // 2 == k + 32, pltpu.roll(big[1, k], 2 * k + 65, 1), first)
        second = jnp.where(lane // 2 == k, pltpu.roll(big[2, k], 2 * k + 1, 1), second)
        second = jnp.where(
            lane // 2 == k + 32, pltpu.roll(big[3, k], (2 * k + 65) % COLS, 1), second
        )
        return first, second

    zero = jnp.zeros((ROWS, COLS), f32)
    first, second = lax.fori_loop(0, LEVELS, pack, (zero, zero), unroll=LEVELS)
    cols_send[1] = jnp.where(even, first, roll(second, 1))
    cols_send[0] = jnp.where(even, roll(first, -1), second)

    for sign, a, o, lead, _ in neighbours:
        if adjacent(sign):

            @pl.when(lead == 0)
            def _(sign=sign, a=a, o=o):
                deep_edge(sign, a, o).start()

    centre = own[0]
    coef = 0.08 + (0.12 / LEVELS) * centre
    bottom_e = jnp.where(lane == COLS - 1, 0.0, roll(centre, -1))
    bottom_w = jnp.where(lane == 0, 0.0, roll(centre, 1))
    bottom_n = jnp.where(row == ROWS - 1, 0.0, slide(centre, -1))
    bottom_s = jnp.where(row == 0, 0.0, slide(centre, 1))

    def inner(k, carry):
        press, sum_x, sum_y = carry
        depth = lax.convert_element_type(k, f32)
        wet = centre > depth
        wet_e, wet_w = bottom_e > depth, bottom_w > depth
        wet_n, wet_s = bottom_n > depth, bottom_s > depth

        def lateral(cells):
            return (
                jnp.where(wet_e, roll(cells, -1), cells)
                + jnp.where(wet_w, roll(cells, 1), cells)
                + jnp.where(wet_n, slide(cells, -1), cells)
                + jnp.where(wet_s, slide(cells, 1), cells)
                - 4.0 * cells
            )

        x, y, t, s = big[0, k], big[1, k], big[2, k], big[3, k]
        press = press + jnp.where(wet, 0.6 * s - 0.8 * t, 0.0)
        press_x = jnp.where(lane == COLS - 1, 0.0, roll(press, -1)) - jnp.where(
            lane == 0, 0.0, roll(press, 1)
        )
        press_y = jnp.where(row == ROWS - 1, 0.0, slide(press, -1)) - jnp.where(
            row == 0, 0.0, slide(press, 1)
        )
        x_out[k] = x + coef * lateral(x) + CORIOLIS * y - 0.1 * press_x
        y_out[k] = y + coef * lateral(y) - CORIOLIS * x - 0.1 * press_y
        below = centre > depth + 1.0
        up, down = lax.max(k - 1, 0), lax.min(k + 1, LEVELS - 1)
        for i, cells, out in ((2, t, t_out), (3, s, s_out)):
            vertical = (big[i, up] - cells) + jnp.where(below, big[i, down] - cells, 0.0)
            out[k] = cells + coef * lateral(cells) + DIAPYCNAL * vertical
        return press, sum_x + jnp.where(wet, x, 0.0), sum_y + jnp.where(wet, y, 0.0)

    _, sum_x, sum_y = lax.fori_loop(0, LEVELS, inner, (zero, zero, zero), unroll=LEVELS)
    count = jnp.maximum(centre, 1.0)
    mean_x, mean_y = sum_x / count, sum_y / count

    for sign, a, o, lead, _ in neighbours:

        @pl.when(lead == 1)
        def _(sign=sign, a=a, o=o):
            halo(sign, -a, -o).wait_recv()
            halo(sign, a, o).start()
            if adjacent(sign):
                deep_edge(sign, a, o).start()

    for sign, a, o, lead, _ in neighbours:

        @pl.when(lead == 0)
        def _(sign=sign, a=a, o=o):
            halo(sign, -a, -o).wait_recv()

    for sign, a, o, _, _ in neighbours:
        if adjacent(sign):
            deep_edge(sign, -a, -o).wait_recv()

    fields = [[], [], [], []]
    for a in (-2, -1, 0, 1, 2):
        inside = (lat + a >= 0) & (lat + a < lats)
        keep = jnp.where(inside, 1.0, 0.0).astype(f32)
        merged = jnp.where(lane % 32 < EDGE, side_recv[a + 2], side_recv[a + 7])
        for i in range(4):
            middle = own[i] if a == 0 else stack_recv[a + 2, i]
            beside = roll(merged, -(EDGE + 32 * i))
            if i == 0 and a != 0:
                middle, beside = middle * keep, beside * keep
            fields[i].append((middle, beside))
    halo_bottom = fields[0]
    beside = halo_bottom[2][1]
    bottom_ew = jnp.where(
        lane == COLS - 1, roll(beside, -1), jnp.where(lane == 0, roll(beside, 1), 0.0)
    )
    bottom_ns = jnp.where(
        row == ROWS - 1,
        slide(halo_bottom[3][0], -1),
        jnp.where(row == 0, slide(halo_bottom[1][0], 1), 0.0),
    )
    from_west, from_east = cols_recv[0], cols_recv[1]
    first = jnp.where(even, from_east, roll(from_west, 1))
    second = jnp.where(even, roll(from_east, -1), from_west)
    sign_ew = jnp.where(lane == COLS - 1, 1.0, -1.0)
    sign_ns = jnp.where(row == ROWS - 1, 1.0, -1.0)
    t_ew, s_ew = 0.08 * sign_ew, -0.06 * sign_ew
    t_ns, s_ns = 0.08 * sign_ns, -0.06 * sign_ns
    upper = row < ROWS // 2

    def outer(k, carry):
        press_ew, press_ns = carry
        depth = lax.convert_element_type(k, f32)
        wet = centre > depth
        wet_ew, wet_ns = bottom_ew > depth, bottom_ns > depth
        sides = [
            pltpu.roll(source, (COLS - 1 - 2 * (k + base)) % COLS, 1)
            for source, base in ((first, 0), (first, 32), (second, 0), (second, 32))
        ]
        stacks = [
            jnp.where(
                upper,
                jnp.broadcast_to(rows_recv[0, pl.ds(i * LEVELS + k, 1), :], (ROWS, COLS)),
                jnp.broadcast_to(rows_recv[1, pl.ds(i * LEVELS + k, 1), :], (ROWS, COLS)),
            )
            for i in range(4)
        ]

        def lateral(i):
            cells = big[i, k]
            return jnp.where(wet_ew, sides[i] - cells, 0.0) + jnp.where(
                wet_ns, stacks[i] - cells, 0.0
            )

        press_ew = press_ew + jnp.where(wet_ew, t_ew * sides[2] + s_ew * sides[3], 0.0)
        press_ns = press_ns + jnp.where(wet_ns, t_ns * stacks[2] + s_ns * stacks[3], 0.0)
        x_out[k] = x_out[k] + coef * lateral(0) + press_ew
        y_out[k] = y_out[k] + coef * lateral(1) + press_ns
        t_out[k] = jnp.where(wet, t_out[k] + coef * lateral(2), 0.0)
        s_out[k] = jnp.where(wet, s_out[k] + coef * lateral(3), 0.0)
        return press_ew, press_ns

    edge_press = (zero, zero)


    def whole(tiles):
        return jnp.concatenate(
            [jnp.concatenate([m for m, _ in tiles], 0), jnp.concatenate([b for _, b in tiles], 0)], 1
        )

    def turn(cells, shift):
        return pltpu.roll(cells, shift % (2 * COLS), 1)

    def ns(cells):
        return pltpu.roll(cells, cells.shape[0] - 1, 0) - pltpu.roll(cells, 1, 0)

    column, level, flow_x, flow_y = (whole(tiles) for tiles in fields)
    wet = jnp.where(column > 0.0, 1.0, 0.0)
    gain = (WAVE / LEVELS) * column
    level, flow_x, flow_y = wet * level, wet * flow_x, wet * flow_y
    wet_e, wet_w = turn(wet, -1), turn(wet, 1)
    for cycle in range(SUBCYCLES):
        flux_x = gain * flow_x
        part = level - wet * ns(gain * flow_y)
        level = part - wet * (turn(flux_x, -1) - turn(flux_x, 1))
        slope_x = (turn(part, -1) - wet_e * (turn(flux_x, -2) - flux_x)) - (
            turn(part, 1) - wet_w * (flux_x - turn(flux_x, 2))
        )
        flow_x, flow_y = (
            flow_x - gain * slope_x + CORIOLIS * flow_y,
            flow_y - gain * ns(level) - CORIOLIS * flow_x,
        )
        edge_press = lax.fori_loop(4 * cycle, 4 * cycle + 4, outer, edge_press, unroll=4)
        if cycle == 3:
            wet, wet_e, wet_w, gain, level, flow_x, flow_y = (
                cells[ROWS : 4 * ROWS]
                for cells in (wet, wet_e, wet_w, gain, level, flow_x, flow_y)
            )
    level, flow_x, flow_y = (cells[ROWS : 2 * ROWS, :COLS] for cells in (level, flow_x, flow_y))
    flat_out[0] = level
    flat_out[1] = flow_x
    flat_out[2] = flow_y

    add_x, add_y = flow_x - mean_x, flow_y - mean_y

    def finish(k, carry):
        wet = centre > lax.convert_element_type(k, f32)
        x_out[k] = jnp.where(wet, x_out[k] + add_x, 0.0)
        y_out[k] = jnp.where(wet, y_out[k] + add_y, 0.0)
        return carry

    lax.fori_loop(0, LEVELS, finish, 0, unroll=LEVELS)

    for sign, a, o, _, _ in neighbours:
        halo(sign, a, o).wait_send()
        if adjacent(sign):
            deep_edge(sign, a, o).wait_send()


def store(flat, x, y, t, s, *rest):
    outs, sem = rest[:-1], rest[-1]
    sources = [flat.at[i] for i in range(3)] + [x, y, t, s]
    copies = [
        pltpu.make_async_copy(source, out, sem.at[i])
        for i, (source, out) in enumerate(zip(sources, outs))
    ][::-1]
    for copy in copies:
        copy.start()
    for copy in copies:
        copy.wait()


def body(*args):
    flat = jax.ShapeDtypeStruct((ROWS, COLS), f32)
    deep = jax.ShapeDtypeStruct((LEVELS, ROWS, COLS), f32)
    messages = 19
    args = [pltpu.with_memory_space_constraint(arg, pltpu.HBM) for arg in args]
    held = pl.pallas_call(
        kernel,
        out_shape=(pltpu.VMEM((3, ROWS, COLS), f32),)
        + (pltpu.VMEM((LEVELS, ROWS, COLS), f32),) * 4,
        in_specs=[pl.BlockSpec(memory_space=pltpu.HBM)] * 8,
        out_specs=(pl.BlockSpec(memory_space=pltpu.VMEM),) * 5,
        scratch_shapes=[
            pltpu.VMEM((ROWS, COLS), jnp.int32),
            pltpu.VMEM((4, ROWS, COLS), f32),
            pltpu.VMEM((4, LEVELS, ROWS, COLS), f32),
            pltpu.VMEM((ROWS, COLS), f32),
            pltpu.VMEM((10, ROWS, COLS), f32),
            pltpu.VMEM((5, 4, ROWS, COLS), f32),
            pltpu.VMEM((2, 4 * LEVELS, COLS), f32),
            pltpu.VMEM((2, 4 * LEVELS, COLS), f32),
            pltpu.VMEM((2, ROWS, COLS), f32),
            pltpu.VMEM((2, ROWS, COLS), f32),
            pltpu.SemaphoreType.DMA((8,)),
            pltpu.SemaphoreType.DMA((messages,)),
            pltpu.SemaphoreType.DMA((messages,)),
        ],
        compiler_params=pltpu.CompilerParams(
            collective_id=0, has_side_effects=True, vmem_limit_bytes=16 * 1024 * 1024
        ),
        name="step",
    )(*args)
    return pl.pallas_call(
        store,
        out_shape=(flat,) * 3 + (deep,) * 4,
        in_specs=[pl.BlockSpec(memory_space=pltpu.VMEM)] * 5,
        out_specs=(pl.BlockSpec(memory_space=pltpu.HBM),) * 7,
        scratch_shapes=[pltpu.SemaphoreType.DMA((7,))],
        compiler_params=pltpu.CompilerParams(vmem_limit_bytes=1024 * 1024),
        name="store",
    )(*(pltpu.with_memory_space_constraint(cells, pltpu.VMEM) for cells in held))


def solution(mesh):
    flat, deep = P("lat", "lon"), P(None, "lat", "lon")
    return jax.shard_map(
        body,
        mesh=mesh,
        in_specs=(flat,) * 4 + (deep,) * 4,
        out_specs=(flat,) * 3 + (deep,) * 4,
        check_vma=False,
    )
```
